256 devices in a mesh: day: 4 (over y), subj: 64 (over z, x, core).
Axes of the slice: x: 4, y: 4, z: 8, core: 2. Of those that a mesh axis runs over, the one named last changes fastest.
Arguments:
- tile_values: float32 [4, 6144, 128, 128], P('day', 'subj'), may hold values from 0 to 3, as said below
- tile_subject: int32 [4, 6144], P('day', 'subj'), may hold values from 0 to 1
- tile_object: int32 [4, 6144], P('day', 'subj'), may hold values from 0 to 127, as said below
- tile_relation: int32 [4, 6144], P('day', 'subj'), may hold values from 0 to 299
- tile_day: int32 [4, 6144], P('day', 'subj'), may hold values from 0 to 31
- tile_count: int32 [4, 64], P('day', 'subj'), may hold values from 1 to 96, as said below
- object_factor: float32 [16384, 256], P('subj'), may hold values from 0.003 to 0.015, as said below
- relation_factor: float32 [300, 256], replicated, may hold values from 0.003 to 0.005
- day_factor: float32 [128, 256], P('day'), may hold values from 0.003 to 0.015, as said below
Outputs:
- subject_factor: float32 [16384, 256], P('subj')
- object_update: float32 [16384, 256], P('subj')
The draws below stay inside these ranges and needn't reach their ends.
Inputs may be any that keep to these rules, and one draw needn't show every extreme that they name: `tile_count`: each device has 1 to 96 live slots, and some device has exactly 96; slots at or beyond a device's count hold arbitrary finite contents. `tile_object`: all slots of one device (live or not) name at most one object block among the 2 blocks p * 2 to p * 2 + 1 of each subj index p. `tile_values`: nonnegative intensities. `object_factor`: positive entries. `day_factor`: positive entries.
All inputs are finite; a program needn't handle non-finite values. Where the reference program divides by a largest or mean magnitude, that divisor is 1e-20 or more.
Results may differ from the reference program's by a relative error of at most 0.00065.
Values sent between devices are 32-bit elements; how exact they have to be, the bound alone decides.
No kernel may reach another device: no remote copies, remote signals or barrier semaphores. Data moves between devices by JAX's collectives and lax.ppermute only.
A program may use at most 128 MiB of HBM per device.

```python
import math
import jax
import jax.numpy as jnp
import numpy as np
from jax import lax

R = 256
TB = 128
REL = 300
DAYS_DEV = 32
SB_DEV = 2
OB_DEV = 2
TILES_DEV = 96
OBJECTS = 16384
DAYS = 128
TILES = 6144
N_DAY = 4
N_SUBJ = 64


def draw_tile_values(key, part):
    shards = TILES // TILES_DEV
    groups = DAYS // DAYS_DEV
    u = jax.random.uniform(key, (groups, TILES, TB, TB), jnp.float32)
    row = (jnp.arange(TILES) // TILES_DEV).astype(jnp.float32) / max(shards - 1, 1)
    rise = 1.0 + 2.0 * row
    base = u
    return (base * rise[None, :, None, None]).astype(jnp.float32)


def draw_tile_object(key, part):
    shards = TILES // TILES_DEV
    groups = DAYS // DAYS_DEV
    pick = jax.random.randint(jax.random.fold_in(key, 11), (groups, shards, shards), 0, OB_DEV)
    owner = jax.random.randint(jax.random.fold_in(key, 12), (groups, shards, TILES_DEV), 0, shards)
    pick = pick.at[0, 0, shards - 1].set(OB_DEV - 1)
    pick = pick.at[0, 0, 0].set(0)
    owner = owner.at[0, 0, 0].set(shards - 1)
    owner = owner.at[0, 0, 1].set(0)
    within = jnp.take_along_axis(pick, owner, axis=2)
    return (owner * OB_DEV + within).reshape(groups, TILES).astype(jnp.int32)


def draw_tile_count(key, part):
    shards = TILES // TILES_DEV
    groups = DAYS // DAYS_DEV
    draws = jax.random.randint(jax.random.fold_in(key, 21), (groups * shards,), 0, TILES_DEV)
    counts = 1 + draws * draws // TILES_DEV
    where = jax.random.randint(jax.random.fold_in(key, 22), (), 0, groups * shards)
    counts = jnp.where(jnp.arange(groups * shards) == where, TILES_DEV, counts)
    return counts.reshape(groups, shards).astype(jnp.int32)


def rising_factor(key, rows):
    u = jax.random.uniform(key, (rows, R), jnp.float32)
    base = 0.6 + 0.4 * u
    rise = 1.0 + 2.0 * jnp.arange(rows).astype(jnp.float32) / max(rows - 1, 1)
    return (0.005 * base * rise[:, None]).astype(jnp.float32)


def draw_object_factor(key, part):
    return rising_factor(key, OBJECTS)


def draw_day_factor(key, part):
    return rising_factor(key, DAYS)


def place_ends(drawn, stream_key, low, top_value):
    place = [jax.random.randint(jax.random.fold_in(stream_key, axis), (), 0, length) for axis, length in enumerate(drawn.shape)]
    widest = drawn.shape.index(max(drawn.shape))
    next_to = place[:widest] + [(place[widest] + 1) % drawn.shape[widest]] + place[widest + 1:]
    return drawn.at[tuple(place)].set(low).at[tuple(next_to)].set(top_value)


def rank_bounds(amount, lean):
    portions = [(1 << 20) // math.isqrt(rank ** lean) + 1 for rank in range(1, amount + 1)]
    deviation = 1 + sum(portions) // (1 << 30)
    return np.cumsum(np.array([max(1, weight // deviation) for weight in portions]))


def ranked(key, dims, count, lean):
    grid = rank_bounds(count, lean)
    lot = jax.random.randint(jax.random.fold_in(key, 1), dims, 0, int(grid[count - 1]))
    rank = jnp.searchsorted(jnp.asarray(grid, jnp.int32), lot, side="right")
    return jax.random.permutation(jax.random.fold_in(key, 2), count)[rank].astype(jnp.int32)


def setup_inputs(seed: int = 0) -> dict:
    streams_of = jax.random.split(jax.random.key(seed), 10)
    tile_values = draw_tile_values(jax.random.fold_in(streams_of[9], 71), 0)
    tile_subject = place_ends(jax.random.randint(streams_of[1], (N_DAY, TILES), 0, SB_DEV), jax.random.fold_in(streams_of[1], 1), 0, SB_DEV - 1).astype(jnp.int32)
    tile_object = draw_tile_object(jax.random.fold_in(streams_of[9], 71), 0)
    tile_relation = place_ends(ranked(streams_of[3], (N_DAY, TILES), REL, 2), jax.random.fold_in(streams_of[3], 3), 0, REL - 1).astype(jnp.int32)
    tile_day = place_ends(jax.random.randint(streams_of[4], (N_DAY, TILES), 0, DAYS_DEV), jax.random.fold_in(streams_of[4], 1), 0, DAYS_DEV - 1).astype(jnp.int32)
    tile_count = draw_tile_count(jax.random.fold_in(streams_of[9], 71), 0)
    object_factor = draw_object_factor(jax.random.fold_in(streams_of[9], 71), 0)
    relation_factor = jnp.clip(jnp.exp(jax.random.uniform(streams_of[7], (REL, R), jnp.float32, math.log(0.003), math.log(0.005))), 0.003, 0.005)
    day_factor = draw_day_factor(jax.random.fold_in(streams_of[9], 71), 0)
    return dict(tile_values=tile_values, tile_subject=tile_subject, tile_object=tile_object, tile_relation=tile_relation, tile_day=tile_day, tile_count=tile_count, object_factor=object_factor, relation_factor=relation_factor, day_factor=day_factor)


HIGH = lax.Precision.HIGHEST
EPS = 1e-06

def solve_rows(total, gram):
    factor = jnp.linalg.cholesky(gram)
    return jax.scipy.linalg.cho_solve((factor, True), total.T).T

def normalized(raw):
    peak = jnp.max(jnp.abs(raw), axis=0)
    return raw / (peak + EPS)

def reference(tile_values, tile_subject, tile_object, tile_relation, tile_day, tile_count, object_factor, relation_factor, day_factor):
    devices = N_DAY * N_SUBJ
    values = tile_values.reshape(devices, TILES_DEV, TB, TB)
    subject = tile_subject.reshape(devices, TILES_DEV)
    target = tile_object.reshape(devices, TILES_DEV)
    relation = tile_relation.reshape(devices, TILES_DEV)
    moment = tile_day.reshape(devices, TILES_DEV)
    live = (jnp.arange(TILES_DEV)[None, :] < tile_count.reshape(devices, 1)).astype(jnp.float32)
    group = (jnp.arange(devices) // N_SUBJ).astype(jnp.int32)
    shard = (jnp.arange(devices) % N_SUBJ).astype(jnp.int32)
    day_global = moment + group[:, None] * DAYS_DEV
    scale = relation_factor[relation] * day_factor[day_global] * live[:, :, None]
    blocks_b = object_factor.reshape(OB_DEV * N_SUBJ, TB, R)
    gram_obj = jnp.dot(object_factor.T, object_factor, precision=HIGH)
    gram_rel = jnp.dot(relation_factor.T, relation_factor, precision=HIGH)
    gram_day = jnp.dot(day_factor.T, day_factor, precision=HIGH)

    def subject_part(item):
        vals, sub, obj, sc = item
        terms = jnp.einsum('tij,tjr->tir', vals, blocks_b[obj], precision=HIGH) * sc[:, None, :]
        pick = jax.nn.one_hot(sub, SB_DEV, dtype=jnp.float32)
        return jnp.einsum('ts,tir->sir', pick, terms, precision=HIGH).reshape(SB_DEV * TB, R)
    parts = lax.map(subject_part, (values, subject, target, scale))
    subject_total = jnp.sum(parts.reshape(N_DAY, N_SUBJ * SB_DEV * TB, R), axis=0)
    subject_raw = solve_rows(subject_total, gram_obj * gram_rel * gram_day)
    subject_factor = normalized(subject_raw)
    gram_subj = jnp.dot(subject_factor.T, subject_factor, precision=HIGH)
    blocks_a = subject_factor.reshape(N_SUBJ, SB_DEV, TB, R)

    def object_step(carry, item):
        vals, sub, obj, sc, where = item
        left = blocks_a[where][sub]
        terms = jnp.einsum('tij,tir->tjr', vals, left, precision=HIGH) * sc[:, None, :]
        return (carry + jax.ops.segment_sum(terms, obj, OB_DEV * N_SUBJ), None)
    start = jnp.zeros((OB_DEV * N_SUBJ, TB, R), jnp.float32)
    object_total, _ = lax.scan(object_step, start, (values, subject, target, scale, shard))
    object_raw = solve_rows(object_total.reshape(OBJECTS, R), gram_subj * gram_rel * gram_day)
    return (subject_factor, normalized(object_raw))
```

```python
import functools

import jax
import jax.numpy as jnp
from jax import lax
from jax.experimental import pallas as pl
from jax.experimental.pallas import tpu as pltpu
from jax.sharding import PartitionSpec as P

F32 = jnp.float32
BF = jnp.bfloat16
HIGH = lax.Precision.HIGHEST
EPS = 1e-06
LIFT = 65536.0

NZ, NX = 8, 4
N_DAY = 4
SIDE = 128
HALF = 128
CHIP_ROWS = 512
SPLIT_X = 208
SPLIT_Z = CHIP_ROWS - SPLIT_X
BLOCKS = NZ * NX * 4
GROUP = 4


def pairs_z(k):
    return [(s, ((s // 8 + k) % NZ) * 8 + s % 8) for s in range(64)]


def pairs_x(k):
    return [(s, (s // 8) * 8 + ((s // 2 % 4 + k) % NX) * 2 + s % 2) for s in range(64)]


def flip(x, mask):
    return lax.ppermute(x, "subj", [(s, s ^ mask) for s in range(64)])


def flip_day(x, mask):
    return lax.ppermute(x, "day", [(s, s ^ mask) for s in range(N_DAY)])


def ring_gather(v, n, pairs):
    out = [None] * n
    out[0] = v
    h = v.shape[0] // 2
    up = down = v
    for s in range(1, n // 2):
        up = lax.ppermute(up, "subj", pairs(1))
        down = lax.ppermute(down, "subj", pairs(-1))
        out[n - s] = up
        out[s] = down
    far_up = lax.ppermute(up[:h], "subj", pairs(1))
    far_down = lax.ppermute(down[h:], "subj", pairs(-1))
    out[n // 2] = jnp.concatenate([far_up, far_down], 0)
    return out


def ring_scatter(parts, n, pairs):
    far = parts[n // 2]
    h = far.shape[0] // 2
    up = lax.ppermute(far[:h], "subj", pairs(1))
    down = lax.ppermute(far[h:], "subj", pairs(-1))
    for k in range(n // 2 - 1, 0, -1):
        a, b = parts[k], parts[n - k]
        if k == n // 2 - 1:
            up = jnp.concatenate([a[:h] + up, a[h:]], 0)
            down = jnp.concatenate([b[:h], b[h:] + down], 0)
        else:
            up = a + up
            down = b + down
        up = lax.ppermute(up, "subj", pairs(1))
        down = lax.ppermute(down, "subj", pairs(-1))
    return parts[0] + up + down


def day_sum(x):
    return (x + flip_day(x, 1)) + (flip_day(x, 2) + flip_day(x, 3))


def day_gather(x, d):
    parts = [x] + [
        lax.ppermute(x, "day", [(s, (s - k) % N_DAY) for s in range(N_DAY)]) for k in (1, 2, 3)
    ]
    both = jnp.concatenate(parts + parts, 0)
    n = x.shape[0]
    return lax.dynamic_slice_in_dim(both, ((N_DAY - d) % N_DAY) * n, N_DAY * n, 0)


def core_order(c, mine, other, axis):
    return jnp.where(
        c == 0,
        jnp.concatenate([mine, other], axis),
        jnp.concatenate([other, mine], axis),
    )


def to_chip(m, c):
    mine = lax.dynamic_slice_in_dim(m, c * HALF, HALF, 1)
    send = lax.dynamic_slice_in_dim(m, (1 - c) * HALF, HALF, 1)
    return core_order(c, mine, flip(send, 1), 0)


def to_core(u, c):
    rows = CHIP_ROWS // 2
    mine = lax.dynamic_slice_in_dim(u, c * rows, rows, 0)
    send = lax.dynamic_slice_in_dim(u, (1 - c) * rows, rows, 0)
    return core_order(c, mine, flip(send, 1), 1)


def gram_over_subj(m, d):
    quarter = m.shape[1] // N_DAY
    cols = lax.dynamic_slice_in_dim(m, d * quarter, quarter, 1)
    g = jnp.dot(cols.T, m, precision=HIGH)
    g = g + flip(g, 1)
    g = (g + flip(g, 2)) + (flip(g, 4) + flip(g, 6))
    for mask in (8, 16, 32):
        g = g + flip(g, mask)
    return day_gather(g, d)


def inverse_factor(gram):
    low = jnp.linalg.cholesky(gram)
    return lax.linalg.triangular_solve(
        low, jnp.eye(gram.shape[0], dtype=F32), left_side=True, lower=True
    )


def solve_rows(total, inv):
    y = jnp.dot(total, inv.T, precision=HIGH)
    return jnp.dot(y, inv, precision=HIGH)


def split2(x):
    hi = x.astype(BF)
    lo = (x - hi.astype(F32)).astype(BF)
    return hi, lo


def tile_dot(v, w):
    hi, lo = split2(v)
    r = jnp.dot(
        jnp.concatenate([hi, lo], 1), jnp.concatenate([w, w], 0), preferred_element_type=F32
    )
    return r[:, :HALF] + r[:, HALF:]


def subject_kernel(cnt, sub, obj, scale, own, sib, *rest):
    pieces = rest[: NZ + NX]
    out = rest[NZ + NX]
    raw, parts, vals, sems = rest[NZ + NX + 1 :]
    tiles = own.shape[0]
    first = [
        [
            pltpu.make_async_copy(
                pieces[z].at[pl.ds(x * SPLIT_X, SPLIT_X)],
                raw.at[z, x, pl.ds(0, SPLIT_X)],
                sems.at[z],
            )
            for x in range(NX)
        ]
        for z in range(NZ)
    ]
    second = [
        [
            pltpu.make_async_copy(
                pieces[NZ + x].at[pl.ds(z * SPLIT_Z, SPLIT_Z)],
                raw.at[z, x, pl.ds(SPLIT_X, SPLIT_Z)],
                sems.at[z],
            )
            for x in range(NX)
        ]
        for z in range(NZ)
    ]
    for z in range(NZ):
        for copy in first[z] + second[z]:
            copy.start()
    own_copy = pltpu.make_async_copy(own, vals.at[pl.ds(0, tiles)], sems.at[NZ])
    sib_copy = pltpu.make_async_copy(sib, vals.at[pl.ds(tiles, tiles)], sems.at[NZ + 1])
    own_copy.start()
    sib_copy.start()
    out[...] = jnp.zeros_like(out)
    for z in range(NZ):
        for copy in first[z] + second[z]:
            copy.wait()
        for x in range(NX):
            for b in range(4):
                hi, lo = split2(raw[z, x, b * SIDE : (b + 1) * SIDE])
                n = (z * NX + x) * 4 + b
                parts[n, :, :HALF] = hi
                parts[n, :, HALF:] = lo

    def run(base, live):
        def step(g, carry):
            terms = []
            for u in range(GROUP):
                q = base + g * GROUP + u
                terms.append(tile_dot(vals[q], parts[obj[q]]) * scale[pl.ds(q, 1), :])
            for u in range(GROUP):
                out[sub[base + g * GROUP + u]] += terms[u]
            return carry

        lax.fori_loop(0, (live + GROUP - 1) // GROUP, step, 0)

    own_copy.wait()
    run(0, cnt[0])
    sib_copy.wait()
    run(tiles, cnt[1])


def object_kernel(cnt, sub, obj, scale, rows, own, sib, *rest):
    outs = rest[: NZ + NX]
    acc, parts, vals, sems = rest[NZ + NX :]
    tiles = own.shape[0]
    own_copy = pltpu.make_async_copy(own, vals.at[pl.ds(0, tiles)], sems.at[0])
    sib_copy = pltpu.make_async_copy(sib, vals.at[pl.ds(tiles, tiles)], sems.at[1])
    own_copy.start()
    sib_copy.start()
    acc[...] = jnp.zeros_like(acc)
    for b in range(4):
        hi, lo = split2(rows[b])
        parts[b, :, :HALF] = hi
        parts[b, :, HALF:] = lo

    def run(base, live):
        def step(g, carry):
            terms = []
            for u in range(GROUP):
                q = base + g * GROUP + u
                terms.append(tile_dot(vals[q].T, parts[sub[q]]) * scale[pl.ds(q, 1), :])
            for u in range(GROUP):
                at = pl.multiple_of(obj[base + g * GROUP + u] * SIDE, SIDE)
                acc[pl.ds(at, SIDE), :] += terms[u]
            return carry

        lax.fori_loop(0, (live + GROUP - 1) // GROUP, step, 0)

    own_copy.wait()
    run(0, cnt[0])
    sib_copy.wait()
    run(tiles, cnt[1])
    copies = []
    for z in range(NZ):
        for x in range(NX):
            at = (z * NX + x) * CHIP_ROWS
            copies.append(
                pltpu.make_async_copy(
                    acc.at[pl.ds(at, SPLIT_X)], outs[z].at[pl.ds(x * SPLIT_X, SPLIT_X)], sems.at[2]
                )
            )
            copies.append(
                pltpu.make_async_copy(
                    acc.at[pl.ds(at + SPLIT_X, SPLIT_Z)],
                    outs[NZ + x].at[pl.ds(z * SPLIT_Z, SPLIT_Z)],
                    sems.at[2],
                )
            )
    for copy in copies:
        copy.start()
    for copy in copies:
        copy.wait()


SMEM = pl.BlockSpec(memory_space=pltpu.SMEM)
VMEM = pl.BlockSpec(memory_space=pltpu.VMEM)
ANY = pl.BlockSpec(memory_space=pl.ANY)
PARAMS = pltpu.CompilerParams(vmem_limit_bytes=40 << 20)


def subject_terms(cnt, sub, obj, scale, own, sib, pieces):
    return pl.pallas_call(
        subject_kernel,
        in_specs=[SMEM] * 3 + [VMEM] + [ANY] * (2 + NZ + NX),
        out_specs=VMEM,
        out_shape=jax.ShapeDtypeStruct((4, SIDE, HALF), F32),
        scratch_shapes=[
            pltpu.VMEM((NZ, NX, CHIP_ROWS, HALF), F32),
            pltpu.VMEM((BLOCKS, SIDE, 2 * HALF), BF),
            pltpu.VMEM((2 * own.shape[0], SIDE, SIDE), F32),
            pltpu.SemaphoreType.DMA((NZ + 2,)),
        ],
        compiler_params=PARAMS,
        name="subject_terms",
    )(cnt, sub, obj, scale, own, sib, *pieces)


def object_terms(cnt, sub, obj, scale, rows, own, sib):
    return pl.pallas_call(
        object_kernel,
        in_specs=[SMEM] * 3 + [VMEM] * 2 + [ANY] * 2,
        out_specs=[ANY] * (NZ + NX),
        out_shape=[jax.ShapeDtypeStruct((NX * SPLIT_X, HALF), F32)] * NZ
        + [jax.ShapeDtypeStruct((NZ * SPLIT_Z, HALF), F32)] * NX,
        scratch_shapes=[
            pltpu.VMEM((BLOCKS * SIDE, HALF), F32),
            pltpu.VMEM((4, SIDE, 2 * HALF), BF),
            pltpu.VMEM((2 * own.shape[0], SIDE, SIDE), F32),
            pltpu.SemaphoreType.DMA((3,)),
        ],
        compiler_params=PARAMS,
        name="object_terms",
    )(cnt, sub, obj, scale, rows, own, sib)


def body(
    tile_values,
    tile_subject,
    tile_object,
    tile_relation,
    tile_day,
    tile_count,
    object_factor,
    relation_factor,
    day_factor,
):
    s = lax.axis_index("subj")
    d = lax.axis_index("day")
    c = s % 2
    here_x = s // 2 % NX
    here_z = s // 8
    own = tile_values[0]
    tiles = own.shape[0]

    unit = to_chip(object_factor, c)
    by_x = ring_gather(unit[:SPLIT_X], NX, pairs_x)
    by_z = ring_gather(unit[SPLIT_X:], NZ, pairs_z)
    pieces = ring_gather(jnp.concatenate(by_x, 0), NZ, pairs_z) + ring_gather(
        jnp.concatenate(by_z, 0), NX, pairs_x
    )

    sib = flip(own, 1)
    meta = jnp.concatenate(
        [
            tile_subject + 2 * c,
            tile_object,
            tile_relation,
            tile_day,
            jnp.broadcast_to(tile_count, (1, tiles)),
        ],
        0,
    )
    meta2 = flip(meta, 1)
    sub = jnp.concatenate([meta[0], meta2[0]])
    obj = jnp.concatenate([meta[1], meta2[1]])
    rel = jnp.concatenate([meta[2], meta2[2]])
    day = jnp.concatenate([meta[3], meta2[3]])
    cnt = jnp.concatenate([meta[4, :1], meta2[4, :1]])
    p = obj // 2
    off_z = (p // 8 - here_z) % NZ
    off_x = (p // 2 % NX - here_x) % NX
    slot = ((off_z * NX + off_x) * 2 + p % 2) * 2 + obj % 2
    k = jnp.arange(tiles)
    live = jnp.concatenate([k < cnt[0], k < cnt[1]])
    rel_cols = lax.dynamic_slice_in_dim(relation_factor, c * HALF, HALF, 1)
    day_cols = lax.dynamic_slice_in_dim(day_factor, c * HALF, HALF, 1)
    rel_pick = (rel[:, None] == jnp.arange(relation_factor.shape[0])[None, :]).astype(F32)
    day_pick = (day[:, None] == jnp.arange(day_factor.shape[0])[None, :]).astype(F32)
    scale = jnp.dot(rel_pick, rel_cols, precision=HIGH) * jnp.dot(
        day_pick, day_cols, precision=HIGH
    )
    scale = scale * live[:, None].astype(F32)

    days = day_gather(day_factor, d)
    gram_rest = jnp.dot(relation_factor.T, relation_factor, precision=HIGH) * jnp.dot(
        days.T, days, precision=HIGH
    )
    inv_first = inverse_factor(gram_over_subj(object_factor, d) * gram_rest)

    part = subject_terms(cnt, sub, slot, scale, own, sib, pieces)
    total = day_sum(to_core(part.reshape(CHIP_ROWS, HALF), c))
    raw = solve_rows(total, inv_first)
    lifted = raw * LIFT
    rows = to_chip(lifted, c).reshape(4, SIDE, HALF)

    back = object_terms(cnt, sub, slot, scale, rows, own, sib)
    inv_second = inverse_factor(gram_over_subj(lifted, d) * gram_rest)
    by_z = ring_scatter(back[:NZ], NZ, pairs_z)
    by_x = ring_scatter(back[NZ:], NX, pairs_x)
    low = ring_scatter(
        [by_z[k * SPLIT_X : (k + 1) * SPLIT_X] for k in range(NX)], NX, pairs_x
    )
    high = ring_scatter(
        [by_x[k * SPLIT_Z : (k + 1) * SPLIT_Z] for k in range(NZ)], NZ, pairs_z
    )
    total = day_sum(to_core(jnp.concatenate([low, high], 0), c))
    raw_b = solve_rows(total, inv_second)

    tops = jnp.stack([jnp.max(jnp.abs(raw), axis=0), jnp.max(jnp.abs(raw_b), axis=0)])
    spread = jnp.broadcast_to(tops[None], (64,) + tops.shape)
    tops = jnp.max(lax.all_to_all(spread, "subj", 0, 0, tiled=True), axis=0)
    step = tops[0] + EPS
    grown = step * LIFT
    return (raw / step, raw_b * (grown / (tops[1] * grown + EPS)))


def solution(mesh):
    return jax.shard_map(
        body,
        mesh=mesh,
        in_specs=(
            P("day", "subj", None, None),
            P("day", "subj"),
            P("day", "subj"),
            P("day", "subj"),
            P("day", "subj"),
            P("day", "subj"),
            P("subj", None),
            P(),
            P("day", None),
        ),
        out_specs=(P("subj", None), P("subj", None)),
        check_vma=False,
    )
```

```python
import functools

import jax
import jax.numpy as jnp
from jax import lax
from jax.experimental import pallas as pl
from jax.experimental.pallas import tpu as pltpu
from jax.sharding import PartitionSpec as P

F32 = jnp.float32
BF = jnp.bfloat16
HIGH = lax.Precision.HIGHEST
EPS = 1e-06
LIFT = 65536.0

NZ, NX = 8, 4
N_DAY = 4
SIDE = 128
HALF = 128
CHIP_ROWS = 512
SPLIT_X = 208
SPLIT_Z = CHIP_ROWS - SPLIT_X
BLOCKS = NZ * NX * 4
PANEL = 32
GROUP = 4


def pairs_z(k):
    return [(s, ((s // 8 + k) % NZ) * 8 + s % 8) for s in range(64)]


def pairs_x(k):
    return [(s, (s // 8) * 8 + ((s // 2 % 4 + k) % NX) * 2 + s % 2) for s in range(64)]


def flip(x, mask):
    return lax.ppermute(x, "subj", [(s, s ^ mask) for s in range(64)])


def flip_day(x, mask):
    return lax.ppermute(x, "day", [(s, s ^ mask) for s in range(N_DAY)])


def ring_gather(v, n, pairs):
    out = [None] * n
    out[0] = v
    h = v.shape[0] // 2
    up = down = v
    for s in range(1, n // 2):
        up = lax.ppermute(up, "subj", pairs(1))
        down = lax.ppermute(down, "subj", pairs(-1))
        out[n - s] = up
        out[s] = down
    far_up = lax.ppermute(up[:h], "subj", pairs(1))
    far_down = lax.ppermute(down[h:], "subj", pairs(-1))
    out[n // 2] = jnp.concatenate([far_up, far_down], 0)
    return out


def ring_scatter(parts, n, pairs):
    far = parts[n // 2]
    h = far.shape[0] // 2
    up = lax.ppermute(far[:h], "subj", pairs(1))
    down = lax.ppermute(far[h:], "subj", pairs(-1))
    for k in range(n // 2 - 1, 0, -1):
        a, b = parts[k], parts[n - k]
        if k == n // 2 - 1:
            up = jnp.concatenate([a[:h] + up, a[h:]], 0)
            down = jnp.concatenate([b[:h], b[h:] + down], 0)
        else:
            up = a + up
            down = b + down
        up = lax.ppermute(up, "subj", pairs(1))
        down = lax.ppermute(down, "subj", pairs(-1))
    return parts[0] + up + down


def day_sum(x):
    return (x + flip_day(x, 1)) + (flip_day(x, 2) + flip_day(x, 3))


def day_gather(x, d):
    parts = [x] + [
        lax.ppermute(x, "day", [(s, (s - k) % N_DAY) for s in range(N_DAY)]) for k in (1, 2, 3)
    ]
    both = jnp.concatenate(parts + parts, 0)
    n = x.shape[0]
    return lax.dynamic_slice_in_dim(both, ((N_DAY - d) % N_DAY) * n, N_DAY * n, 0)


def core_order(c, mine, other, axis):
    return jnp.where(
        c == 0,
        jnp.concatenate([mine, other], axis),
        jnp.concatenate([other, mine], axis),
    )


def to_chip(m, c):
    mine = lax.dynamic_slice_in_dim(m, c * HALF, HALF, 1)
    send = lax.dynamic_slice_in_dim(m, (1 - c) * HALF, HALF, 1)
    return core_order(c, mine, flip(send, 1), 0)


def to_core(u, c):
    rows = CHIP_ROWS // 2
    mine = lax.dynamic_slice_in_dim(u, c * rows, rows, 0)
    send = lax.dynamic_slice_in_dim(u, (1 - c) * rows, rows, 0)
    return core_order(c, mine, flip(send, 1), 1)


def gram_over_subj(m, d):
    quarter = m.shape[1] // N_DAY
    cols = lax.dynamic_slice_in_dim(m, d * quarter, quarter, 1)
    g = jnp.dot(cols.T, m, precision=HIGH)
    g = g + flip(g, 1)
    g = (g + flip(g, 2)) + (flip(g, 4) + flip(g, 6))
    for mask in (8, 16, 32):
        g = g + flip(g, mask)
    return day_gather(g, d)


def exact_dot(a, b):
    return jnp.dot(a, b, precision=HIGH, preferred_element_type=F32)


def unit_matrix(n):
    i = lax.broadcasted_iota(jnp.int32, (n, n), 0)
    return (i == lax.broadcasted_iota(jnp.int32, (n, n), 1)).astype(F32)


def block_inverse(block):
    n = block.shape[0]
    wide = jnp.concatenate([block, unit_matrix(n)], 1)
    place = lax.broadcasted_iota(jnp.int32, wide.shape, 0)
    for p in range(0, n, 8):
        cols = [jnp.broadcast_to(wide[:, p + j : p + j + 1], wide.shape) for j in range(8)]
        for j in range(8):
            k = p + j
            pivot = cols[j][k : k + 1, :]
            r = lax.rsqrt(pivot)
            r = r * (1.5 - 0.5 * (pivot * r) * r)
            col = cols[j] * r
            row = wide[k : k + 1, :] * r
            below = jnp.where(place > k, col, 0.0)
            wide = jnp.where(place == k, row, wide - below * row)
            for t in range(j + 1, 8):
                cols[t] = cols[t] - below * col[p + t : p + t + 1, :]
    return wide[:, n:]


def factor_kernel(gram, out, work):
    n = gram.shape[0]
    work[...] = gram[...]
    out[...] = unit_matrix(n)
    for b in range(0, n, PANEL):
        e = b + PANEL
        inv = block_inverse(work[b:e, b:e])
        used = -(-e // 128) * 128
        top = exact_dot(inv, out[b:e, :used])
        out[b:e, :used] = top
        if e < n:
            panel = lax.dot_general(
                work[e:n, b:e], inv, (((1,), (1,)), ((), ())), precision=HIGH,
                preferred_element_type=F32,
            )
            work[e:n, e:n] -= lax.dot_general(
                panel, panel, (((1,), (1,)), ((), ())), precision=HIGH,
                preferred_element_type=F32,
            )
            out[e:n, :used] -= exact_dot(panel, top)


def inverse_factor(gram):
    return pl.pallas_call(
        factor_kernel,
        out_shape=jax.ShapeDtypeStruct(gram.shape, F32),
        scratch_shapes=[pltpu.VMEM(gram.shape, F32)],
        name="inverse_factor",
    )(gram)


def solve_rows(total, inv):
    y = jnp.dot(total, inv.T, precision=HIGH)
    return jnp.dot(y, inv, precision=HIGH)


def split2(x):
    hi = x.astype(BF)
    lo = (x - hi.astype(F32)).astype(BF)
    return hi, lo


def tile_dot(v, w):
    hi, lo = split2(v)
    r = jnp.dot(
        jnp.concatenate([hi, lo], 1), jnp.concatenate([w, w], 0), preferred_element_type=F32
    )
    return r[:, :HALF] + r[:, HALF:]


def subject_kernel(cnt, sub, obj, scale, own, sib, *rest):
    pieces = rest[: NZ + NX]
    out = rest[NZ + NX]
    raw, parts, vals, sems = rest[NZ + NX + 1 :]
    tiles = own.shape[0]
    first = [
        [
            pltpu.make_async_copy(
                pieces[z].at[pl.ds(x * SPLIT_X, SPLIT_X)],
                raw.at[z, x, pl.ds(0, SPLIT_X)],
                sems.at[z],
            )
            for x in range(NX)
        ]
        for z in range(NZ)
    ]
    second = [
        [
            pltpu.make_async_copy(
                pieces[NZ + x].at[pl.ds(z * SPLIT_Z, SPLIT_Z)],
                raw.at[z, x, pl.ds(SPLIT_X, SPLIT_Z)],
                sems.at[z],
            )
            for x in range(NX)
        ]
        for z in range(NZ)
    ]
    for z in range(NZ):
        for copy in first[z] + second[z]:
            copy.start()
    own_copy = pltpu.make_async_copy(own, vals.at[pl.ds(0, tiles)], sems.at[NZ])
    sib_copy = pltpu.make_async_copy(sib, vals.at[pl.ds(tiles, tiles)], sems.at[NZ + 1])
    own_copy.start()
    sib_copy.start()
    out[...] = jnp.zeros_like(out)
    for z in range(NZ):
        for copy in first[z] + second[z]:
            copy.wait()
        for x in range(NX):
            for b in range(4):
                hi, lo = split2(raw[z, x, b * SIDE : (b + 1) * SIDE])
                n = (z * NX + x) * 4 + b
                parts[n, :, :HALF] = hi
                parts[n, :, HALF:] = lo

    def run(base, live):
        def step(g, carry):
            terms = []
            for u in range(GROUP):
                q = base + g * GROUP + u
                terms.append(tile_dot(vals[q], parts[obj[q]]) * scale[pl.ds(q, 1), :])
            for u in range(GROUP):
                out[sub[base + g * GROUP + u]] += terms[u]
            return carry

        lax.fori_loop(0, (live + GROUP - 1) // GROUP, step, 0)

    own_copy.wait()
    run(0, cnt[0])
    sib_copy.wait()
    run(tiles, cnt[1])


def object_kernel(cnt, sub, obj, scale, rows, own, sib, *rest):
    outs = rest[: NZ + NX]
    acc, parts, vals, sems = rest[NZ + NX :]
    tiles = own.shape[0]
    own_copy = pltpu.make_async_copy(own, vals.at[pl.ds(0, tiles)], sems.at[0])
    sib_copy = pltpu.make_async_copy(sib, vals.at[pl.ds(tiles, tiles)], sems.at[1])
    own_copy.start()
    sib_copy.start()
    acc[...] = jnp.zeros_like(acc)
    for b in range(4):
        hi, lo = split2(rows[b])
        parts[b, :, :HALF] = hi
        parts[b, :, HALF:] = lo

    def run(base, live):
        def step(g, carry):
            terms = []
            for u in range(GROUP):
                q = base + g * GROUP + u
                terms.append(tile_dot(vals[q].T, parts[sub[q]]) * scale[pl.ds(q, 1), :])
            for u in range(GROUP):
                at = pl.multiple_of(obj[base + g * GROUP + u] * SIDE, SIDE)
                acc[pl.ds(at, SIDE), :] += terms[u]
            return carry

        lax.fori_loop(0, (live + GROUP - 1) // GROUP, step, 0)

    own_copy.wait()
    run(0, cnt[0])
    sib_copy.wait()
    run(tiles, cnt[1])
    copies = []
    for z in range(NZ):
        for x in range(NX):
            at = (z * NX + x) * CHIP_ROWS
            copies.append(
                pltpu.make_async_copy(
                    acc.at[pl.ds(at, SPLIT_X)], outs[z].at[pl.ds(x * SPLIT_X, SPLIT_X)], sems.at[2]
                )
            )
            copies.append(
                pltpu.make_async_copy(
                    acc.at[pl.ds(at + SPLIT_X, SPLIT_Z)],
                    outs[NZ + x].at[pl.ds(z * SPLIT_Z, SPLIT_Z)],
                    sems.at[2],
                )
            )
    for copy in copies:
        copy.start()
    for copy in copies:
        copy.wait()


SMEM = pl.BlockSpec(memory_space=pltpu.SMEM)
VMEM = pl.BlockSpec(memory_space=pltpu.VMEM)
ANY = pl.BlockSpec(memory_space=pl.ANY)
PARAMS = pltpu.CompilerParams(vmem_limit_bytes=40 << 20)


def subject_terms(cnt, sub, obj, scale, own, sib, pieces):
    return pl.pallas_call(
        subject_kernel,
        in_specs=[SMEM] * 3 + [VMEM] + [ANY] * (2 + NZ + NX),
        out_specs=VMEM,
        out_shape=jax.ShapeDtypeStruct((4, SIDE, HALF), F32),
        scratch_shapes=[
            pltpu.VMEM((NZ, NX, CHIP_ROWS, HALF), F32),
            pltpu.VMEM((BLOCKS, SIDE, 2 * HALF), BF),
            pltpu.VMEM((2 * own.shape[0], SIDE, SIDE), F32),
            pltpu.SemaphoreType.DMA((NZ + 2,)),
        ],
        compiler_params=PARAMS,
        name="subject_terms",
    )(cnt, sub, obj, scale, own, sib, *pieces)


def object_terms(cnt, sub, obj, scale, rows, own, sib):
    return pl.pallas_call(
        object_kernel,
        in_specs=[SMEM] * 3 + [VMEM] * 2 + [ANY] * 2,
        out_specs=[ANY] * (NZ + NX),
        out_shape=[jax.ShapeDtypeStruct((NX * SPLIT_X, HALF), F32)] * NZ
        + [jax.ShapeDtypeStruct((NZ * SPLIT_Z, HALF), F32)] * NX,
        scratch_shapes=[
            pltpu.VMEM((BLOCKS * SIDE, HALF), F32),
            pltpu.VMEM((4, SIDE, 2 * HALF), BF),
            pltpu.VMEM((2 * own.shape[0], SIDE, SIDE), F32),
            pltpu.SemaphoreType.DMA((3,)),
        ],
        compiler_params=PARAMS,
        name="object_terms",
    )(cnt, sub, obj, scale, rows, own, sib)


def body(
    tile_values,
    tile_subject,
    tile_object,
    tile_relation,
    tile_day,
    tile_count,
    object_factor,
    relation_factor,
    day_factor,
):
    s = lax.axis_index("subj")
    d = lax.axis_index("day")
    c = s % 2
    here_x = s // 2 % NX
    here_z = s // 8
    own = tile_values[0]
    tiles = own.shape[0]

    unit = to_chip(object_factor, c)
    by_x = ring_gather(unit[:SPLIT_X], NX, pairs_x)
    by_z = ring_gather(unit[SPLIT_X:], NZ, pairs_z)
    pieces = ring_gather(jnp.concatenate(by_x, 0), NZ, pairs_z) + ring_gather(
        jnp.concatenate(by_z, 0), NX, pairs_x
    )

    sib = flip(own, 1)
    meta = jnp.concatenate(
        [
            tile_subject + 2 * c,
            tile_object,
            tile_relation,
            tile_day,
            jnp.broadcast_to(tile_count, (1, tiles)),
        ],
        0,
    )
    meta2 = flip(meta, 1)
    sub = jnp.concatenate([meta[0], meta2[0]])
    obj = jnp.concatenate([meta[1], meta2[1]])
    rel = jnp.concatenate([meta[2], meta2[2]])
    day = jnp.concatenate([meta[3], meta2[3]])
    cnt = jnp.concatenate([meta[4, :1], meta2[4, :1]])
    p = obj // 2
    off_z = (p // 8 - here_z) % NZ
    off_x = (p // 2 % NX - here_x) % NX
    slot = ((off_z * NX + off_x) * 2 + p % 2) * 2 + obj % 2
    k = jnp.arange(tiles)
    live = jnp.concatenate([k < cnt[0], k < cnt[1]])
    rel_cols = lax.dynamic_slice_in_dim(relation_factor, c * HALF, HALF, 1)
    day_cols = lax.dynamic_slice_in_dim(day_factor, c * HALF, HALF, 1)
    rel_pick = (rel[:, None] == jnp.arange(relation_factor.shape[0])[None, :]).astype(F32)
    day_pick = (day[:, None] == jnp.arange(day_factor.shape[0])[None, :]).astype(F32)
    scale = jnp.dot(rel_pick, rel_cols, precision=HIGH) * jnp.dot(
        day_pick, day_cols, precision=HIGH
    )
    scale = scale * live[:, None].astype(F32)

    days = day_gather(day_factor, d)
    gram_rest = jnp.dot(relation_factor.T, relation_factor, precision=HIGH) * jnp.dot(
        days.T, days, precision=HIGH
    )
    gram_first = gram_over_subj(object_factor, d) * gram_rest

    part = subject_terms(cnt, sub, slot, scale, own, sib, pieces)
    part, gram_first = lax.optimization_barrier((part, gram_first))
    total = day_sum(to_core(part.reshape(CHIP_ROWS, HALF), c))
    inv_first = inverse_factor(gram_first)
    raw = solve_rows(total, inv_first)
    lifted = raw * LIFT
    rows = to_chip(lifted, c).reshape(4, SIDE, HALF)

    back = object_terms(cnt, sub, slot, scale, rows, own, sib)
    gram_second = gram_over_subj(lifted, d) * gram_rest
    by_z = ring_scatter(back[:NZ], NZ, pairs_z)
    by_x = ring_scatter(back[NZ:], NX, pairs_x)
    low = ring_scatter(
        [by_z[k * SPLIT_X : (k + 1) * SPLIT_X] for k in range(NX)], NX, pairs_x
    )
    high = ring_scatter(
        [by_x[k * SPLIT_Z : (k + 1) * SPLIT_Z] for k in range(NZ)], NZ, pairs_z
    )
    low, high, gram_second = lax.optimization_barrier((low, high, gram_second))
    total = day_sum(to_core(jnp.concatenate([low, high], 0), c))
    inv_second = inverse_factor(gram_second)
    raw_b = solve_rows(total, inv_second)

    tops = jnp.stack([jnp.max(jnp.abs(raw), axis=0), jnp.max(jnp.abs(raw_b), axis=0)])
    spread = jnp.broadcast_to(tops[None], (64,) + tops.shape)
    tops = jnp.max(lax.all_to_all(spread, "subj", 0, 0, tiled=True), axis=0)
    step = tops[0] + EPS
    grown = step * LIFT
    return (raw / step, raw_b * (grown / (tops[1] * grown + EPS)))


def solution(mesh):
    return jax.shard_map(
        body,
        mesh=mesh,
        in_specs=(
            P("day", "subj", None, None),
            P("day", "subj"),
            P("day", "subj"),
            P("day", "subj"),
            P("day", "subj"),
            P("day", "subj"),
            P("subj", None),
            P(),
            P("day", None),
        ),
        out_specs=(P("subj", None), P("subj", None)),
        check_vma=False,
    )
```

```python
import functools

import jax
import jax.numpy as jnp
from jax import lax
from jax.experimental import pallas as pl
from jax.experimental.pallas import tpu as pltpu
from jax.sharding import PartitionSpec as P

F32 = jnp.float32
BF = jnp.bfloat16
HIGH = lax.Precision.HIGHEST
EPS = 1e-06
LIFT = 65536.0

NZ, NX = 8, 4
N_DAY = 4
SIDE = 128
HALF = 128
CHIP_ROWS = 512
SPLIT_X = 240
SPLIT_Z = CHIP_ROWS - SPLIT_X
BLOCKS = NZ * NX * 4
PANEL = 32
GROUP = 4


def pairs_z(k):
    return [(s, ((s // 8 + k) % NZ) * 8 + s % 8) for s in range(64)]


def pairs_x(k):
    return [(s, (s // 8) * 8 + ((s // 2 % 4 + k) % NX) * 2 + s % 2) for s in range(64)]


def flip(x, mask):
    return lax.ppermute(x, "subj", [(s, s ^ mask) for s in range(64)])


def flip_day(x, mask):
    return lax.ppermute(x, "day", [(s, s ^ mask) for s in range(N_DAY)])


def ring_gather(v, n, pairs, side=None):
    side = side or Side()
    out = [None] * n
    out[0] = v
    h = v.shape[0] // 2
    up = down = v
    for s in range(1, n // 2):
        side.start()
        up = lax.ppermute(up, "subj", pairs(1))
        down = lax.ppermute(down, "subj", pairs(-1))
        up, down = side.finish(up, down)
        out[n - s] = up
        out[s] = down
    side.start()
    far_up = lax.ppermute(up[:h], "subj", pairs(1))
    far_down = lax.ppermute(down[h:], "subj", pairs(-1))
    far_up, far_down = side.finish(far_up, far_down)
    out[n // 2] = jnp.concatenate([far_up, far_down], 0)
    return out


def ring_scatter(parts, n, pairs, side=None):
    side = side or Side()
    far = parts[n // 2]
    h = far.shape[0] // 2
    side.start()
    up = lax.ppermute(far[:h], "subj", pairs(1))
    down = lax.ppermute(far[h:], "subj", pairs(-1))
    up, down = side.finish(up, down)
    for k in range(n // 2 - 1, 0, -1):
        a, b = parts[k], parts[n - k]
        if k == n // 2 - 1:
            up = jnp.concatenate([a[:h] + up, a[h:]], 0)
            down = jnp.concatenate([b[:h], b[h:] + down], 0)
        else:
            up = a + up
            down = b + down
        side.start()
        up = lax.ppermute(up, "subj", pairs(1))
        down = lax.ppermute(down, "subj", pairs(-1))
        up, down = side.finish(up, down)
    return parts[0] + up + down


class Side:
    def __init__(self, steps=(), value=None):
        self.steps = list(steps)
        self.value = value
        self.moved = None

    def start(self):
        if self.steps:
            self.moved = self.steps[0][0](self.value)

    def finish(self, *ring):
        if not self.steps:
            return ring
        ring, self.moved, self.value = lax.optimization_barrier((ring, self.moved, self.value))
        self.value = self.steps.pop(0)[1](self.value, self.moved)
        return ring

    def drain(self):
        while self.steps:
            self.start()
            self.value = self.steps.pop(0)[1](self.value, self.moved)
        return self.value


def add_steps(masks):
    return [
        (lambda g, m=m: flip(g, m), lambda g, moved: g + moved) for m in masks
    ]


def day_join(mine, moved, late):
    return jnp.where(
        late == 1, jnp.concatenate([moved, mine], 0), jnp.concatenate([mine, moved], 0)
    )


def day_sum(x):
    return (x + flip_day(x, 1)) + (flip_day(x, 2) + flip_day(x, 3))


def core_order(c, mine, other, axis):
    return jnp.where(
        c == 0,
        jnp.concatenate([mine, other], axis),
        jnp.concatenate([other, mine], axis),
    )


def to_chip(m, c):
    mine = lax.dynamic_slice_in_dim(m, c * HALF, HALF, 1)
    send = lax.dynamic_slice_in_dim(m, (1 - c) * HALF, HALF, 1)
    return core_order(c, mine, flip(send, 1), 0)


def to_core(u, c):
    rows = CHIP_ROWS // 2
    mine = lax.dynamic_slice_in_dim(u, c * rows, rows, 0)
    send = lax.dynamic_slice_in_dim(u, (1 - c) * rows, rows, 0)
    return core_order(c, mine, flip(send, 1), 1)


def gram_part(m, d):
    quarter = m.shape[1] // N_DAY
    cols = lax.dynamic_slice_in_dim(m, d * quarter, quarter, 1)
    return jnp.dot(cols.T, m, precision=HIGH)


def exact_dot(a, b):
    return jnp.dot(a, b, precision=HIGH, preferred_element_type=F32)


def unit_matrix(n):
    i = lax.broadcasted_iota(jnp.int32, (n, n), 0)
    return (i == lax.broadcasted_iota(jnp.int32, (n, n), 1)).astype(F32)


def block_inverse(block):
    n = block.shape[0]
    wide = jnp.concatenate([block, unit_matrix(n)], 1)
    place = lax.broadcasted_iota(jnp.int32, wide.shape, 0)
    for p in range(0, n, 8):
        cols = [jnp.broadcast_to(wide[:, p + j : p + j + 1], wide.shape) for j in range(8)]
        for j in range(8):
            k = p + j
            pivot = cols[j][k : k + 1, :]
            r = lax.rsqrt(pivot)
            r = r * (1.5 - 0.5 * (pivot * r) * r)
            col = cols[j] * r
            row = wide[k : k + 1, :] * r
            below = jnp.where(place > k, col, 0.0)
            wide = jnp.where(place == k, row, wide - below * row)
            for t in range(j + 1, 8):
                cols[t] = cols[t] - below * col[p + t : p + t + 1, :]
    return wide[:, n:]


def factor_kernel(gram, out, work):
    n = gram.shape[0]
    work[...] = gram[...]
    out[...] = unit_matrix(n)
    for b in range(0, n, PANEL):
        e = b + PANEL
        inv = block_inverse(work[b:e, b:e])
        used = -(-e // 128) * 128
        top = exact_dot(inv, out[b:e, :used])
        out[b:e, :used] = top
        if e < n:
            panel = lax.dot_general(
                work[e:n, b:e], inv, (((1,), (1,)), ((), ())), precision=HIGH,
                preferred_element_type=F32,
            )
            work[e:n, e:n] -= lax.dot_general(
                panel, panel, (((1,), (1,)), ((), ())), precision=HIGH,
                preferred_element_type=F32,
            )
            out[e:n, :used] -= exact_dot(panel, top)


def inverse_factor(gram):
    return pl.pallas_call(
        factor_kernel,
        out_shape=jax.ShapeDtypeStruct(gram.shape, F32),
        scratch_shapes=[pltpu.VMEM(gram.shape, F32)],
        name="inverse_factor",
    )(gram)


def solve_rows(total, inv):
    y = jnp.dot(total, inv.T, precision=HIGH)
    return jnp.dot(y, inv, precision=HIGH)


def split2(x):
    hi = x.astype(BF)
    lo = (x - hi.astype(F32)).astype(BF)
    return hi, lo


def tile_dot(v, w):
    hi, lo = split2(v)
    r = jnp.dot(
        jnp.concatenate([hi, lo], 1), jnp.concatenate([w, w], 0), preferred_element_type=F32
    )
    return r[:, :HALF] + r[:, HALF:]


def subject_kernel(cnt, sub, obj, scale, own, sib, *rest):
    pieces = rest[: NZ + NX]
    out = rest[NZ + NX]
    raw, parts, vals, sems = rest[NZ + NX + 1 :]
    tiles = own.shape[0]
    first = [
        [
            pltpu.make_async_copy(
                pieces[z].at[pl.ds(x * SPLIT_X, SPLIT_X)],
                raw.at[z, x, pl.ds(0, SPLIT_X)],
                sems.at[z],
            )
            for x in range(NX)
        ]
        for z in range(NZ)
    ]
    second = [
        [
            pltpu.make_async_copy(
                pieces[NZ + x].at[pl.ds(z * SPLIT_Z, SPLIT_Z)],
                raw.at[z, x, pl.ds(SPLIT_X, SPLIT_Z)],
                sems.at[z],
            )
            for x in range(NX)
        ]
        for z in range(NZ)
    ]
    for z in range(NZ):
        for copy in first[z] + second[z]:
            copy.start()
    own_copy = pltpu.make_async_copy(own, vals.at[pl.ds(0, tiles)], sems.at[NZ])
    sib_copy = pltpu.make_async_copy(sib, vals.at[pl.ds(tiles, tiles)], sems.at[NZ + 1])
    own_copy.start()
    sib_copy.start()
    out[...] = jnp.zeros_like(out)
    for z in range(NZ):
        for copy in first[z] + second[z]:
            copy.wait()
        for x in range(NX):
            for b in range(4):
                hi, lo = split2(raw[z, x, b * SIDE : (b + 1) * SIDE])
                n = (z * NX + x) * 4 + b
                parts[n, :, :HALF] = hi
                parts[n, :, HALF:] = lo

    def run(base, live):
        def step(g, carry):
            terms = []
            for u in range(GROUP):
                q = base + g * GROUP + u
                terms.append(tile_dot(vals[q], parts[obj[q]]) * scale[pl.ds(q, 1), :])
            for u in range(GROUP):
                out[sub[base + g * GROUP + u]] += terms[u]
            return carry

        lax.fori_loop(0, (live + GROUP - 1) // GROUP, step, 0)

    own_copy.wait()
    run(0, cnt[0])
    sib_copy.wait()
    run(tiles, cnt[1])


def object_kernel(cnt, sub, obj, scale, rows, own, sib, *rest):
    outs = rest[: NZ + NX]
    acc, parts, vals, sems = rest[NZ + NX :]
    tiles = own.shape[0]
    own_copy = pltpu.make_async_copy(own, vals.at[pl.ds(0, tiles)], sems.at[0])
    sib_copy = pltpu.make_async_copy(sib, vals.at[pl.ds(tiles, tiles)], sems.at[1])
    own_copy.start()
    sib_copy.start()
    acc[...] = jnp.zeros_like(acc)
    for b in range(4):
        hi, lo = split2(rows[b])
        parts[b, :, :HALF] = hi
        parts[b, :, HALF:] = lo

    def run(base, live):
        def step(g, carry):
            terms = []
            for u in range(GROUP):
                q = base + g * GROUP + u
                terms.append(tile_dot(vals[q].T, parts[sub[q]]) * scale[pl.ds(q, 1), :])
            for u in range(GROUP):
                at = pl.multiple_of(obj[base + g * GROUP + u] * SIDE, SIDE)
                acc[pl.ds(at, SIDE), :] += terms[u]
            return carry

        lax.fori_loop(0, (live + GROUP - 1) // GROUP, step, 0)

    own_copy.wait()
    run(0, cnt[0])
    sib_copy.wait()
    run(tiles, cnt[1])
    copies = []
    for z in range(NZ):
        for x in range(NX):
            at = (z * NX + x) * CHIP_ROWS
            copies.append(
                pltpu.make_async_copy(
                    acc.at[pl.ds(at, SPLIT_X)], outs[z].at[pl.ds(x * SPLIT_X, SPLIT_X)], sems.at[2]
                )
            )
            copies.append(
                pltpu.make_async_copy(
                    acc.at[pl.ds(at + SPLIT_X, SPLIT_Z)],
                    outs[NZ + x].at[pl.ds(z * SPLIT_Z, SPLIT_Z)],
                    sems.at[2],
                )
            )
    for copy in copies:
        copy.start()
    for copy in copies:
        copy.wait()


SMEM = pl.BlockSpec(memory_space=pltpu.SMEM)
VMEM = pl.BlockSpec(memory_space=pltpu.VMEM)
ANY = pl.BlockSpec(memory_space=pl.ANY)
PARAMS = pltpu.CompilerParams(vmem_limit_bytes=40 << 20)


def subject_terms(cnt, sub, obj, scale, own, sib, pieces):
    return pl.pallas_call(
        subject_kernel,
        in_specs=[SMEM] * 3 + [VMEM] + [ANY] * (2 + NZ + NX),
        out_specs=VMEM,
        out_shape=jax.ShapeDtypeStruct((4, SIDE, HALF), F32),
        scratch_shapes=[
            pltpu.VMEM((NZ, NX, CHIP_ROWS, HALF), F32),
            pltpu.VMEM((BLOCKS, SIDE, 2 * HALF), BF),
            pltpu.VMEM((2 * own.shape[0], SIDE, SIDE), F32),
            pltpu.SemaphoreType.DMA((NZ + 2,)),
        ],
        compiler_params=PARAMS,
        name="subject_terms",
    )(cnt, sub, obj, scale, own, sib, *pieces)


def object_terms(cnt, sub, obj, scale, rows, own, sib):
    return pl.pallas_call(
        object_kernel,
        in_specs=[SMEM] * 3 + [VMEM] * 2 + [ANY] * 2,
        out_specs=[ANY] * (NZ + NX),
        out_shape=[jax.ShapeDtypeStruct((NX * SPLIT_X, HALF), F32)] * NZ
        + [jax.ShapeDtypeStruct((NZ * SPLIT_Z, HALF), F32)] * NX,
        scratch_shapes=[
            pltpu.VMEM((BLOCKS * SIDE, HALF), F32),
            pltpu.VMEM((4, SIDE, 2 * HALF), BF),
            pltpu.VMEM((2 * own.shape[0], SIDE, SIDE), F32),
            pltpu.SemaphoreType.DMA((3,)),
        ],
        compiler_params=PARAMS,
        name="object_terms",
    )(cnt, sub, obj, scale, rows, own, sib)


def body(
    tile_values,
    tile_subject,
    tile_object,
    tile_relation,
    tile_day,
    tile_count,
    object_factor,
    relation_factor,
    day_factor,
):
    s = lax.axis_index("subj")
    d = lax.axis_index("day")
    c = s % 2
    here_x = s // 2 % NX
    here_z = s // 8
    own = tile_values[0]
    tiles = own.shape[0]

    meta = jnp.concatenate(
        [
            tile_subject + 2 * c,
            tile_object,
            tile_relation,
            tile_day,
            jnp.broadcast_to(tile_count, (1, tiles)),
        ],
        0,
    )
    unit = to_chip(object_factor, c)
    meta2 = flip(meta, 1)
    gram = gram_part(object_factor, d)
    gram = gram + flip(gram, 1)
    unit, meta2, gram = lax.optimization_barrier((unit, meta2, gram))

    sib = flip(own, 1)
    side = Side(
        [
            (lambda g: (), lambda g, moved: g),
            (lambda g: sib, lambda g, moved: g),
        ]
        + add_steps((2, 4, 8, 16, 32)),
        gram,
    )
    by_x = ring_gather(unit[:SPLIT_X], NX, pairs_x)
    by_z = ring_gather(unit[SPLIT_X:], NZ, pairs_z, side)
    pieces = ring_gather(jnp.concatenate(by_x, 0), NZ, pairs_z, side) + ring_gather(
        jnp.concatenate(by_z, 0), NX, pairs_x
    )
    gram = side.drain()
    days = day_factor
    for mask, late in ((1, d % 2), (2, d // 2)):
        n = gram.shape[0]
        moved = flip_day(jnp.concatenate([gram, days], 0), mask)
        gram = day_join(gram, moved[:n], late)
        days = day_join(days, moved[n:], late)

    sub = jnp.concatenate([meta[0], meta2[0]])
    obj = jnp.concatenate([meta[1], meta2[1]])
    rel = jnp.concatenate([meta[2], meta2[2]])
    day = jnp.concatenate([meta[3], meta2[3]])
    cnt = jnp.concatenate([meta[4, :1], meta2[4, :1]])
    p = obj // 2
    off_z = (p // 8 - here_z) % NZ
    off_x = (p // 2 % NX - here_x) % NX
    slot = ((off_z * NX + off_x) * 2 + p % 2) * 2 + obj % 2
    k = jnp.arange(tiles)
    live = jnp.concatenate([k < cnt[0], k < cnt[1]])
    rel_cols = lax.dynamic_slice_in_dim(relation_factor, c * HALF, HALF, 1)
    day_cols = lax.dynamic_slice_in_dim(day_factor, c * HALF, HALF, 1)
    rel_pick = (rel[:, None] == jnp.arange(relation_factor.shape[0])[None, :]).astype(F32)
    day_pick = (day[:, None] == jnp.arange(day_factor.shape[0])[None, :]).astype(F32)
    scale = jnp.dot(rel_pick, rel_cols, precision=HIGH) * jnp.dot(
        day_pick, day_cols, precision=HIGH
    )
    scale = scale * live[:, None].astype(F32)

    gram_rest = jnp.dot(relation_factor.T, relation_factor, precision=HIGH) * jnp.dot(
        days.T, days, precision=HIGH
    )
    gram_first = gram * gram_rest

    part = subject_terms(cnt, sub, slot, scale, own, sib, pieces)
    part, gram_first = lax.optimization_barrier((part, gram_first))
    total = day_sum(to_core(part.reshape(CHIP_ROWS, HALF), c))
    inv_first = inverse_factor(gram_first)
    raw = solve_rows(total, inv_first)
    lifted = raw * LIFT
    rows = to_chip(lifted, c).reshape(4, SIDE, HALF)

    gram = gram_part(lifted, d)
    rows, gram = lax.optimization_barrier((rows, gram))
    moved = flip(gram, 1)
    back = object_terms(cnt, sub, slot, scale, rows, own, sib)
    back, gram, moved = lax.optimization_barrier((back, gram, moved))
    side = Side(add_steps((2, 4, 8, 16, 32)), gram + moved)
    by_z = ring_scatter(back[:NZ], NZ, pairs_z, side)
    by_x = ring_scatter(back[NZ:], NX, pairs_x)
    low = ring_scatter(
        [by_z[k * SPLIT_X : (k + 1) * SPLIT_X] for k in range(NX)], NX, pairs_x
    )
    side.steps += [
        (lambda g: flip_day(g, 1), lambda g, m: day_join(g, m, d % 2)),
        (lambda g: flip_day(g, 2), lambda g, m: day_join(g, m, d // 2)),
    ]
    high = ring_scatter(
        [by_x[k * SPLIT_Z : (k + 1) * SPLIT_Z] for k in range(NZ)], NZ, pairs_z, side
    )
    gram_second = side.drain() * gram_rest
    low, high, gram_second = lax.optimization_barrier((low, high, gram_second))
    total = day_sum(to_core(jnp.concatenate([low, high], 0), c))
    inv_second = inverse_factor(gram_second)
    raw_b = solve_rows(total, inv_second)

    tops = jnp.stack([jnp.max(jnp.abs(raw), axis=0), jnp.max(jnp.abs(raw_b), axis=0)])
    spread = jnp.broadcast_to(tops[None], (64,) + tops.shape)
    tops = jnp.max(lax.all_to_all(spread, "subj", 0, 0, tiled=True), axis=0)
    step = tops[0] + EPS
    grown = step * LIFT
    return (raw / step, raw_b * (grown / (tops[1] * grown + EPS)))


def solution(mesh):
    return jax.shard_map(
        body,
        mesh=mesh,
        in_specs=(
            P("day", "subj", None, None),
            P("day", "subj"),
            P("day", "subj"),
            P("day", "subj"),
            P("day", "subj"),
            P("day", "subj"),
            P("subj", None),
            P(),
            P("day", None),
        ),
        out_specs=(P("subj", None), P("subj", None)),
        check_vma=False,
    )
```

```python
import functools

import jax
import jax.numpy as jnp
from jax import lax
from jax.experimental import pallas as pl
from jax.experimental.pallas import tpu as pltpu
from jax.sharding import PartitionSpec as P

F32 = jnp.float32
BF = jnp.bfloat16
HIGH = lax.Precision.HIGHEST
EPS = 1e-06
LIFT = 65536.0

NZ, NX = 8, 4
N_DAY = 4
SIDE = 128
HALF = 128
CHIP_ROWS = 512
SPLIT_X = 240
SPLIT_Z = CHIP_ROWS - SPLIT_X
BLOCKS = NZ * NX * 4
PANEL = 32
GROUP = 12
CHUNK = 48


def pairs_z(k):
    return [(s, ((s // 8 + k) % NZ) * 8 + s % 8) for s in range(64)]


def pairs_x(k):
    return [(s, (s // 8) * 8 + ((s // 2 % 4 + k) % NX) * 2 + s % 2) for s in range(64)]


def flip(x, mask):
    return lax.ppermute(x, "subj", [(s, s ^ mask) for s in range(64)])


def flip_day(x, mask):
    return lax.ppermute(x, "day", [(s, s ^ mask) for s in range(N_DAY)])


def ring_gather(v, n, pairs, side=None):
    side = side or Side()
    out = [None] * n
    out[0] = v
    h = v.shape[0] // 2
    up = down = v
    for s in range(1, n // 2):
        side.start()
        up = lax.ppermute(up, "subj", pairs(1))
        down = lax.ppermute(down, "subj", pairs(-1))
        up, down = side.finish(up, down)
        out[n - s] = up
        out[s] = down
    side.start()
    far_up = lax.ppermute(up[:h], "subj", pairs(1))
    far_down = lax.ppermute(down[h:], "subj", pairs(-1))
    far_up, far_down = side.finish(far_up, far_down)
    out[n // 2] = jnp.concatenate([far_up, far_down], 0)
    return out


def ring_scatter(parts, n, pairs, side=None):
    side = side or Side()
    far = parts[n // 2]
    h = far.shape[0] // 2
    side.start()
    up = lax.ppermute(far[:h], "subj", pairs(1))
    down = lax.ppermute(far[h:], "subj", pairs(-1))
    up, down = side.finish(up, down)
    for k in range(n // 2 - 1, 0, -1):
        a, b = parts[k], parts[n - k]
        if k == n // 2 - 1:
            up = jnp.concatenate([a[:h] + up, a[h:]], 0)
            down = jnp.concatenate([b[:h], b[h:] + down], 0)
        else:
            up = a + up
            down = b + down
        side.start()
        up = lax.ppermute(up, "subj", pairs(1))
        down = lax.ppermute(down, "subj", pairs(-1))
        up, down = side.finish(up, down)
    return parts[0] + up + down


class Side:
    def __init__(self, steps=(), value=None):
        self.steps = list(steps)
        self.value = value
        self.moved = None

    def start(self):
        if self.steps:
            self.moved = self.steps[0][0](self.value)

    def finish(self, *ring):
        if not self.steps:
            return ring
        ring, self.moved, self.value = lax.optimization_barrier((ring, self.moved, self.value))
        self.value = self.steps.pop(0)[1](self.value, self.moved)
        return ring

    def drain(self):
        while self.steps:
            self.start()
            self.value = self.steps.pop(0)[1](self.value, self.moved)
        return self.value


def add_steps(masks):
    return [
        (lambda g, m=m: flip(g, m), lambda g, moved: g + moved) for m in masks
    ]


def day_join(mine, moved, late):
    return jnp.where(
        late == 1, jnp.concatenate([moved, mine], 0), jnp.concatenate([mine, moved], 0)
    )


def day_sum(x):
    return (x + flip_day(x, 1)) + (flip_day(x, 2) + flip_day(x, 3))


def core_order(c, mine, other, axis):
    return jnp.where(
        c == 0,
        jnp.concatenate([mine, other], axis),
        jnp.concatenate([other, mine], axis),
    )


def to_chip(m, c):
    mine = lax.dynamic_slice_in_dim(m, c * HALF, HALF, 1)
    send = lax.dynamic_slice_in_dim(m, (1 - c) * HALF, HALF, 1)
    return core_order(c, mine, flip(send, 1), 0)


def to_core(u, c):
    rows = CHIP_ROWS // 2
    mine = lax.dynamic_slice_in_dim(u, c * rows, rows, 0)
    send = lax.dynamic_slice_in_dim(u, (1 - c) * rows, rows, 0)
    return core_order(c, mine, flip(send, 1), 1)


def gram_part(m, d):
    quarter = m.shape[1] // N_DAY
    cols = lax.dynamic_slice_in_dim(m, d * quarter, quarter, 1)
    return jnp.dot(cols.T, m, precision=HIGH)


def exact_dot(a, b):
    return jnp.dot(a, b, precision=HIGH, preferred_element_type=F32)


def unit_matrix(n):
    i = lax.broadcasted_iota(jnp.int32, (n, n), 0)
    return (i == lax.broadcasted_iota(jnp.int32, (n, n), 1)).astype(F32)


def block_inverse(block):
    n = block.shape[0]
    wide = jnp.concatenate([block, unit_matrix(n)], 1)
    place = lax.broadcasted_iota(jnp.int32, wide.shape, 0)
    for p in range(0, n, 8):
        cols = [jnp.broadcast_to(wide[:, p + j : p + j + 1], wide.shape) for j in range(8)]
        for j in range(8):
            k = p + j
            pivot = cols[j][k : k + 1, :]
            r = lax.rsqrt(pivot)
            r = r * (1.5 - 0.5 * (pivot * r) * r)
            col = cols[j] * r
            row = wide[k : k + 1, :] * r
            below = jnp.where(place > k, col, 0.0)
            wide = jnp.where(place == k, row, wide - below * row)
            for t in range(j + 1, 8):
                cols[t] = cols[t] - below * col[p + t : p + t + 1, :]
    return wide[:, n:]


def factor_kernel(gram, out, work):
    n = gram.shape[0]
    work[...] = gram[...]
    out[...] = unit_matrix(n)
    for b in range(0, n, PANEL):
        e = b + PANEL
        inv = block_inverse(work[b:e, b:e])
        used = -(-e // 128) * 128
        top = exact_dot(inv, out[b:e, :used])
        out[b:e, :used] = top
        if e < n:
            panel = lax.dot_general(
                work[e:n, b:e], inv, (((1,), (1,)), ((), ())), precision=HIGH,
                preferred_element_type=F32,
            )
            work[e:n, e:n] -= lax.dot_general(
                panel, panel, (((1,), (1,)), ((), ())), precision=HIGH,
                preferred_element_type=F32,
            )
            out[e:n, :used] -= exact_dot(panel, top)


def inverse_factor(gram):
    return pl.pallas_call(
        factor_kernel,
        out_shape=jax.ShapeDtypeStruct(gram.shape, F32),
        scratch_shapes=[pltpu.VMEM(gram.shape, F32)],
        name="inverse_factor",
    )(gram)


def solve_rows(total, inv):
    y = jnp.dot(total, inv.T, precision=HIGH)
    return jnp.dot(y, inv, precision=HIGH)


def split2(x):
    hi = x.astype(BF)
    lo = (x - hi.astype(F32)).astype(BF)
    return hi, lo


def tile_dot(v, w):
    hi, lo = split2(v)
    r = jnp.dot(
        jnp.concatenate([hi, lo], 1), jnp.concatenate([w, w], 0), preferred_element_type=F32
    )
    return r[:, :HALF] + r[:, HALF:]


def tile_copies(own, sib, vals, sems, first_sem):
    tiles = own.shape[0]
    copies = []
    for core, src in enumerate((own, sib)):
        for at in range(0, tiles, CHUNK):
            copies.append(
                pltpu.make_async_copy(
                    src.at[pl.ds(at, CHUNK)],
                    vals.at[pl.ds(core * tiles + at, CHUNK)],
                    sems.at[first_sem + len(copies)],
                )
            )
    return copies


def subject_kernel(cnt, sub, obj, scale, own, sib, *rest):
    pieces = rest[: NZ + NX]
    out = rest[NZ + NX]
    raw, parts, vals, sems = rest[NZ + NX + 1 :]
    tiles = own.shape[0]
    first = [
        [
            pltpu.make_async_copy(
                pieces[z].at[pl.ds(x * SPLIT_X, SPLIT_X)],
                raw.at[z, x, pl.ds(0, SPLIT_X)],
                sems.at[z],
            )
            for x in range(NX)
        ]
        for z in range(NZ)
    ]
    second = [
        [
            pltpu.make_async_copy(
                pieces[NZ + x].at[pl.ds(z * SPLIT_Z, SPLIT_Z)],
                raw.at[z, x, pl.ds(SPLIT_X, SPLIT_Z)],
                sems.at[z],
            )
            for x in range(NX)
        ]
        for z in range(NZ)
    ]
    for z in range(NZ):
        for copy in first[z] + second[z]:
            copy.start()
    copies = tile_copies(own, sib, vals, sems, NZ)
    for copy in copies:
        copy.start()
    out[...] = jnp.zeros_like(out)
    for z in range(NZ):
        for copy in first[z] + second[z]:
            copy.wait()
        for x in range(NX):
            for b in range(4):
                hi, lo = split2(raw[z, x, b * SIDE : (b + 1) * SIDE])
                n = (z * NX + x) * 4 + b
                parts[n, :, :HALF] = hi
                parts[n, :, HALF:] = lo

    def run(base, live):
        def step(g, carry):
            terms = []
            for u in range(GROUP):
                q = base + g * GROUP + u
                terms.append(tile_dot(vals[q], parts[obj[q]]) * scale[pl.ds(q, 1), :])
            for u in range(GROUP):
                out[sub[base + g * GROUP + u]] += terms[u]
            return carry

        lax.fori_loop(0, (live + GROUP - 1) // GROUP, step, 0)

    for k, copy in enumerate(copies):
        copy.wait()
        core, first_tile = divmod(k * CHUNK, tiles)
        run(k * CHUNK, jnp.clip(cnt[core] - first_tile, 0, CHUNK))


def object_kernel(cnt, sub, obj, scale, rows, own, sib, acc, parts, vals, sems):
    tiles = own.shape[0]
    copies = tile_copies(own, sib, vals, sems, 0)
    for copy in copies:
        copy.start()
    acc[...] = jnp.zeros_like(acc)
    for b in range(4):
        hi, lo = split2(rows[b])
        parts[b, :, :HALF] = hi
        parts[b, :, HALF:] = lo

    def run(base, live):
        def step(g, carry):
            terms = []
            for u in range(GROUP):
                q = base + g * GROUP + u
                terms.append(tile_dot(vals[q].T, parts[sub[q]]) * scale[pl.ds(q, 1), :])
            for u in range(GROUP):
                at = pl.multiple_of(obj[base + g * GROUP + u] * SIDE, SIDE)
                acc[pl.ds(at, SIDE), :] += terms[u]
            return carry

        lax.fori_loop(0, (live + GROUP - 1) // GROUP, step, 0)

    for k, copy in enumerate(copies):
        copy.wait()
        core, first_tile = divmod(k * CHUNK, tiles)
        run(k * CHUNK, jnp.clip(cnt[core] - first_tile, 0, CHUNK))


SMEM = pl.BlockSpec(memory_space=pltpu.SMEM)
VMEM = pl.BlockSpec(memory_space=pltpu.VMEM)
ANY = pl.BlockSpec(memory_space=pl.ANY)
PARAMS = pltpu.CompilerParams(vmem_limit_bytes=40 << 20)


def subject_terms(cnt, sub, obj, scale, own, sib, pieces):
    return pl.pallas_call(
        subject_kernel,
        in_specs=[SMEM] * 3 + [VMEM] + [ANY] * (2 + NZ + NX),
        out_specs=VMEM,
        out_shape=jax.ShapeDtypeStruct((4, SIDE, HALF), F32),
        scratch_shapes=[
            pltpu.VMEM((NZ, NX, CHIP_ROWS, HALF), F32),
            pltpu.VMEM((BLOCKS, SIDE, 2 * HALF), BF),
            pltpu.VMEM((2 * own.shape[0], SIDE, SIDE), F32),
            pltpu.SemaphoreType.DMA((NZ + 2 * own.shape[0] // CHUNK,)),
        ],
        compiler_params=PARAMS,
        name="subject_terms",
    )(cnt, sub, obj, scale, own, sib, *pieces)


def object_terms(cnt, sub, obj, scale, rows, own, sib):
    return pl.pallas_call(
        object_kernel,
        in_specs=[SMEM] * 3 + [VMEM] * 2 + [ANY] * 2,
        out_specs=VMEM,
        out_shape=jax.ShapeDtypeStruct((BLOCKS * SIDE, HALF), F32),
        scratch_shapes=[
            pltpu.VMEM((4, SIDE, 2 * HALF), BF),
            pltpu.VMEM((2 * own.shape[0], SIDE, SIDE), F32),
            pltpu.SemaphoreType.DMA((2 * own.shape[0] // CHUNK,)),
        ],
        compiler_params=PARAMS,
        name="object_terms",
    )(cnt, sub, obj, scale, rows, own, sib)


def body(
    tile_values,
    tile_subject,
    tile_object,
    tile_relation,
    tile_day,
    tile_count,
    object_factor,
    relation_factor,
    day_factor,
):
    s = lax.axis_index("subj")
    d = lax.axis_index("day")
    c = s % 2
    here_x = s // 2 % NX
    here_z = s // 8
    own = tile_values[0]
    tiles = own.shape[0]

    meta = jnp.concatenate(
        [
            tile_subject + 2 * c,
            tile_object,
            tile_relation,
            tile_day,
            jnp.broadcast_to(tile_count, (1, tiles)),
        ],
        0,
    )
    unit = to_chip(object_factor, c)
    meta2 = flip(meta, 1)

    def swap(g):
        return flip(lax.optimization_barrier((own, g))[0], 1)

    side = Side(
        add_steps((1, 2, 4, 8, 16, 32)) + [(swap, lambda g, moved: (g, moved))],
        gram_part(object_factor, d),
    )
    by_x = ring_gather(unit[:SPLIT_X], NX, pairs_x)
    by_z = ring_gather(unit[SPLIT_X:], NZ, pairs_z, side)
    pieces = ring_gather(jnp.concatenate(by_x, 0), NZ, pairs_z, side) + ring_gather(
        jnp.concatenate(by_z, 0), NX, pairs_x
    )
    gram, sib = side.drain()
    days = day_factor
    for mask, late in ((1, d % 2), (2, d // 2)):
        n = gram.shape[0]
        moved = flip_day(jnp.concatenate([gram, days], 0), mask)
        gram = day_join(gram, moved[:n], late)
        days = day_join(days, moved[n:], late)

    sub = jnp.concatenate([meta[0], meta2[0]])
    obj = jnp.concatenate([meta[1], meta2[1]])
    rel = jnp.concatenate([meta[2], meta2[2]])
    day = jnp.concatenate([meta[3], meta2[3]])
    cnt = jnp.concatenate([meta[4, :1], meta2[4, :1]])
    p = obj // 2
    off_z = (p // 8 - here_z) % NZ
    off_x = (p // 2 % NX - here_x) % NX
    slot = ((off_z * NX + off_x) * 2 + p % 2) * 2 + obj % 2
    k = jnp.arange(tiles)
    live = jnp.concatenate([k < cnt[0], k < cnt[1]])
    rel_cols = lax.dynamic_slice_in_dim(relation_factor, c * HALF, HALF, 1)
    day_cols = lax.dynamic_slice_in_dim(day_factor, c * HALF, HALF, 1)
    rel_pick = (rel[:, None] == jnp.arange(relation_factor.shape[0])[None, :]).astype(F32)
    day_pick = (day[:, None] == jnp.arange(day_factor.shape[0])[None, :]).astype(F32)
    scale = jnp.dot(rel_pick, rel_cols, precision=HIGH) * jnp.dot(
        day_pick, day_cols, precision=HIGH
    )
    scale = scale * live[:, None].astype(F32)

    gram_rest = jnp.dot(relation_factor.T, relation_factor, precision=HIGH) * jnp.dot(
        days.T, days, precision=HIGH
    )
    gram_first = gram * gram_rest

    part = subject_terms(cnt, sub, slot, scale, own, sib, pieces)
    part, gram_first = lax.optimization_barrier((part, gram_first))
    total = day_sum(to_core(part.reshape(CHIP_ROWS, HALF), c))
    inv_first = inverse_factor(gram_first)
    raw = solve_rows(total, inv_first)
    lifted = raw * LIFT
    rows = to_chip(lifted, c).reshape(4, SIDE, HALF)

    gram = gram_part(lifted, d)
    gram = gram + flip(gram, 1)
    rows, gram = lax.optimization_barrier((rows, gram))
    moved = [flip(gram, mask) for mask in (2, 4, 6)]
    back = object_terms(cnt, sub, slot, scale, rows, own, sib)
    back, gram, moved = lax.optimization_barrier((back, gram, moved))
    back = back.reshape(NZ, NX, CHIP_ROWS, HALF)
    to_z = [back[z, :, :SPLIT_X].reshape(NX * SPLIT_X, HALF) for z in range(NZ)]
    to_x = [back[:, x, SPLIT_X:].reshape(NZ * SPLIT_Z, HALF) for x in range(NX)]
    side = Side(
        add_steps((8, 16, 32))
        + [
            (lambda g: flip_day(g, 1), lambda g, m: day_join(g, m, d % 2)),
            (lambda g: flip_day(g, 2), lambda g, m: day_join(g, m, d // 2)),
        ],
        (gram + moved[0]) + (moved[1] + moved[2]),
    )
    by_z = ring_scatter(to_z, NZ, pairs_z, side)
    by_x = ring_scatter(to_x, NX, pairs_x)
    low = ring_scatter(
        [by_z[k * SPLIT_X : (k + 1) * SPLIT_X] for k in range(NX)], NX, pairs_x
    )
    high = ring_scatter(
        [by_x[k * SPLIT_Z : (k + 1) * SPLIT_Z] for k in range(NZ)], NZ, pairs_z, side
    )
    gram_second = side.drain() * gram_rest
    low, high, gram_second = lax.optimization_barrier((low, high, gram_second))
    total = day_sum(to_core(jnp.concatenate([low, high], 0), c))
    inv_second = inverse_factor(gram_second)
    raw_b = solve_rows(total, inv_second)

    tops = jnp.stack([jnp.max(jnp.abs(raw), axis=0), jnp.max(jnp.abs(raw_b), axis=0)])
    spread = jnp.broadcast_to(tops[None], (64,) + tops.shape)
    tops = jnp.max(lax.all_to_all(spread, "subj", 0, 0, tiled=True), axis=0)
    step = tops[0] + EPS
    grown = step * LIFT
    return (raw / step, raw_b * (grown / (tops[1] * grown + EPS)))


def solution(mesh):
    return jax.shard_map(
        body,
        mesh=mesh,
        in_specs=(
            P("day", "subj", None, None),
            P("day", "subj"),
            P("day", "subj"),
            P("day", "subj"),
            P("day", "subj"),
            P("day", "subj"),
            P("subj", None),
            P(),
            P("day", None),
        ),
        out_specs=(P("subj", None), P("subj", None)),
        check_vma=False,
    )
```

```python
import functools

import jax
import jax.numpy as jnp
from jax import lax
from jax.experimental import pallas as pl
from jax.experimental.pallas import tpu as pltpu
from jax.sharding import PartitionSpec as P

F32 = jnp.float32
BF = jnp.bfloat16
HIGH = lax.Precision.HIGHEST
EPS = 1e-06
LIFT = 65536.0

NZ, NX = 8, 4
N_DAY = 4
SIDE = 128
HALF = 128
CHIP_ROWS = 512
SPLIT_X = 224
SPLIT_Z = CHIP_ROWS - SPLIT_X
BLOCKS = NZ * NX * 4
PANEL = 32
GROUP = 12
CHUNK = 48
ROW_SEM = 4


def pairs_z(k):
    return [(s, ((s // 8 + k) % NZ) * 8 + s % 8) for s in range(64)]


def pairs_x(k):
    return [(s, (s // 8) * 8 + ((s // 2 % 4 + k) % NX) * 2 + s % 2) for s in range(64)]


def flip(x, mask):
    return lax.ppermute(x, "subj", [(s, s ^ mask) for s in range(64)])


def flip_day(x, mask):
    return lax.ppermute(x, "day", [(s, s ^ mask) for s in range(N_DAY)])


def step(moves, *keep):
    got = [
        lax.ppermute(v, "subj", pairs) if axis == "subj" else flip_day(v, pairs)
        for v, axis, pairs in moves
    ]
    return lax.optimization_barrier((got, keep))


def xup(v):
    return (v, "subj", pairs_x(1))


def xdown(v):
    return (v, "subj", pairs_x(-1))


def zup(v):
    return (v, "subj", pairs_z(1))


def zdown(v):
    return (v, "subj", pairs_z(-1))


def mate(v, mask):
    return (v, "subj", [(s, s ^ mask) for s in range(64)])


def day_mate(v, mask):
    return (v, "day", mask)


def cut(v):
    h = v.shape[0] // 2
    return v[:h], v[h:]


def gather_rows(unit, gram, own, d, days):
    a, b = unit[:SPLIT_X], unit[SPLIT_X:]
    (au, ad, bu1, bd1, g), (a, b, gram) = step(
        [xup(a), xdown(a), zup(b), zdown(b), mate(gram, 1)], a, b, gram
    )
    gram = gram + g
    (at, ab, bu2, bd2, g), (gram,) = step(
        [xup(cut(au)[0]), xdown(cut(ad)[1]), zup(bu1), zdown(bd1), mate(gram, 2)], gram
    )
    gram = gram + g
    (bu3, bd3, g), (gram,) = step([zup(bu2), zdown(bd2), mate(gram, 4)], gram)
    gram = gram + g
    (bt, bb, g), (gram,) = step([zup(cut(bu3)[0]), zdown(cut(bd3)[1]), mate(gram, 8)], gram)
    gram = gram + g
    a = jnp.concatenate([a, ad, at, ab, au], 0)
    low = jnp.concatenate([b, bd1, bd2, bd3], 0)
    high = jnp.concatenate([bt, bb, bu3, bu2, bu1], 0)
    a, low, high, gram = lax.optimization_barrier((a, low, high, gram))
    (au1, ad1, lu, ld, g), (a, low, high, gram, own) = step(
        [zup(a), zdown(a), xup(low), xdown(low), mate(gram, 16)], a, low, high, gram, own
    )
    gram = gram + g
    (au2, ad2, hu, hd, g), (lu, gram, own) = step(
        [zup(au1), zdown(ad1), xup(high), xdown(high), mate(gram, 32)], lu, gram, own
    )
    gram = gram + g
    (au3, ad3, lf, hf, sib), (gram,) = step(
        [zup(au2), zdown(ad2), xup(lu), xdown(hd), mate(own, 1)], gram
    )
    n = gram.shape[0]
    (at, ab, g), (gram,) = step(
        [zup(cut(au3)[0]), zdown(cut(ad3)[1]), day_mate(jnp.concatenate([gram, days], 0), 1)],
        gram,
    )
    gram = day_join(gram, g[:n], d % 2)
    days = day_join(days, g[n:], d % 2)
    g = flip_day(jnp.concatenate([gram, days], 0), 2)
    gram = day_join(gram, g[: 2 * n], d // 2)
    days = day_join(days, g[2 * n :], d // 2)
    pieces = []
    for z, v in ((0, a), (1, ad1), (2, ad2), (3, ad3), (5, au3), (6, au2), (7, au1)):
        pieces.append((v, [(z, x, 0) for x in range(NX)]))
    pieces.append((at, [(4, 0, 0), (4, 1, 0)]))
    pieces.append((ab, [(4, 2, 0), (4, 3, 0)]))
    for x, v, first in (
        (0, low, 0), (3, lu, 0), (1, ld, 0), (2, lf, 0),
        (0, high, 4), (3, hu, 4), (1, hd, 4), (2, hf, 4),
    ):
        pieces.append((v, [(first + z, x, SPLIT_X) for z in range(4)]))
    return pieces, sib, gram, days


def scatter_rows(back, gram, d):
    def to_z(z):
        return back[z, :, :SPLIT_X].reshape(NX * SPLIT_X, HALF)

    def to_x(x, first):
        return back[first : first + 4, x, SPLIT_X:].reshape(4 * SPLIT_Z, HALF)

    far_top, far_low = cut(to_z(4))
    (u, v, lu, hd, g), (gram, late_up, late_down) = step(
        [zup(far_top), zdown(far_low), xup(to_x(2, 0)), xdown(to_x(2, 4)), mate(gram, 8)],
        gram, to_x(1, 4), to_x(3, 0),
    )
    gram = gram + g
    p, q = to_z(3), to_z(5)
    p = jnp.concatenate([cut(p)[0] + u, cut(p)[1]], 0)
    q = jnp.concatenate([cut(q)[0], cut(q)[1] + v], 0)
    (u, v, lu, hd, g), (gram, late_up, late_down) = step(
        [zup(p), zdown(q), xup(to_x(1, 0) + lu), xdown(to_x(3, 4) + hd), mate(gram, 16)],
        gram, late_up, late_down,
    )
    gram = gram + g
    (u, v, hu, ld, g), (gram, lu, hd) = step(
        [zup(to_z(2) + u), zdown(to_z(6) + v), xup(late_up), xdown(late_down), mate(gram, 32)],
        gram, lu, hd,
    )
    gram = gram + g
    low = to_x(0, 0) + lu + ld
    high = to_x(0, 4) + hu + hd
    b = [low[k * SPLIT_Z : (k + 1) * SPLIT_Z] for k in range(4)]
    b += [high[k * SPLIT_Z : (k + 1) * SPLIT_Z] for k in range(4)]
    (u, v, bu, bv, g), (gram, b) = step(
        [
            zup(to_z(1) + u), zdown(to_z(7) + v),
            zup(cut(b[4])[0]), zdown(cut(b[4])[1]), day_mate(gram, 1),
        ],
        gram, b,
    )
    gram = day_join(gram, g, d % 2)
    a = to_z(0) + u + v
    a = [a[k * SPLIT_X : (k + 1) * SPLIT_X] for k in range(NX)]
    p = jnp.concatenate([cut(b[3])[0] + bu, cut(b[3])[1]], 0)
    q = jnp.concatenate([cut(b[5])[0], cut(b[5])[1] + bv], 0)
    (bu, bv, u, v, g), (gram, a, b) = step(
        [zup(p), zdown(q), xup(cut(a[2])[0]), xdown(cut(a[2])[1]), day_mate(gram, 2)], gram, a, b
    )
    gram = day_join(gram, g, d // 2)
    p = jnp.concatenate([cut(a[1])[0] + u, cut(a[1])[1]], 0)
    q = jnp.concatenate([cut(a[3])[0], cut(a[3])[1] + v], 0)
    (bu, bv, u, v), (a, b) = step(
        [zup(b[2] + bu), zdown(b[6] + bv), xup(p), xdown(q)], a, b
    )
    a = a[0] + u + v
    (bu, bv), (a, b) = step([zup(b[1] + bu), zdown(b[7] + bv)], a, b)
    return jnp.concatenate([a, b[0] + bu + bv], 0), gram


def day_join(mine, moved, late):
    return jnp.where(
        late == 1, jnp.concatenate([moved, mine], 0), jnp.concatenate([mine, moved], 0)
    )


def day_sum(x):
    return (x + flip_day(x, 1)) + (flip_day(x, 2) + flip_day(x, 3))


def core_order(c, mine, other, axis):
    return jnp.where(
        c == 0,
        jnp.concatenate([mine, other], axis),
        jnp.concatenate([other, mine], axis),
    )


def to_chip(m, c):
    mine = lax.dynamic_slice_in_dim(m, c * HALF, HALF, 1)
    send = lax.dynamic_slice_in_dim(m, (1 - c) * HALF, HALF, 1)
    return core_order(c, mine, flip(send, 1), 0)


def to_core(u, c):
    rows = CHIP_ROWS // 2
    mine = lax.dynamic_slice_in_dim(u, c * rows, rows, 0)
    send = lax.dynamic_slice_in_dim(u, (1 - c) * rows, rows, 0)
    return core_order(c, mine, flip(send, 1), 1)


def gram_part(m, d):
    quarter = m.shape[1] // N_DAY
    cols = lax.dynamic_slice_in_dim(m, d * quarter, quarter, 1)
    return jnp.dot(cols.T, m, precision=HIGH)


def exact_dot(a, b):
    return jnp.dot(a, b, precision=HIGH, preferred_element_type=F32)


def unit_matrix(n):
    i = lax.broadcasted_iota(jnp.int32, (n, n), 0)
    return (i == lax.broadcasted_iota(jnp.int32, (n, n), 1)).astype(F32)


def block_inverse(block):
    n = block.shape[0]
    wide = jnp.concatenate([block, unit_matrix(n)], 1)
    place = lax.broadcasted_iota(jnp.int32, wide.shape, 0)
    for p in range(0, n, 8):
        cols = [jnp.broadcast_to(wide[:, p + j : p + j + 1], wide.shape) for j in range(8)]
        for j in range(8):
            k = p + j
            pivot = cols[j][k : k + 1, :]
            r = lax.rsqrt(pivot)
            r = r * (1.5 - 0.5 * (pivot * r) * r)
            col = cols[j] * r
            row = wide[k : k + 1, :] * r
            below = jnp.where(place > k, col, 0.0)
            wide = jnp.where(place == k, row, wide - below * row)
            for t in range(j + 1, 8):
                cols[t] = cols[t] - below * col[p + t : p + t + 1, :]
    return wide[:, n:]


def factor_kernel(gram, out, work):
    n = gram.shape[0]
    work[...] = gram[...]
    out[...] = unit_matrix(n)
    for b in range(0, n, PANEL):
        e = b + PANEL
        inv = block_inverse(work[b:e, b:e])
        used = -(-e // 128) * 128
        top = exact_dot(inv, out[b:e, :used])
        out[b:e, :used] = top
        if e < n:
            panel = lax.dot_general(
                work[e:n, b:e], inv, (((1,), (1,)), ((), ())), precision=HIGH,
                preferred_element_type=F32,
            )
            work[e:n, e:n] -= lax.dot_general(
                panel, panel, (((1,), (1,)), ((), ())), precision=HIGH,
                preferred_element_type=F32,
            )
            out[e:n, :used] -= exact_dot(panel, top)


def inverse_factor(gram):
    return pl.pallas_call(
        factor_kernel,
        out_shape=jax.ShapeDtypeStruct(gram.shape, F32),
        scratch_shapes=[pltpu.VMEM(gram.shape, F32)],
        name="inverse_factor",
    )(gram)


def solve_rows(total, inv):
    y = jnp.dot(total, inv.T, precision=HIGH)
    return jnp.dot(y, inv, precision=HIGH)


def split2(x):
    hi = x.astype(BF)
    lo = (x - hi.astype(F32)).astype(BF)
    return hi, lo


def tile_dot(v, w):
    hi, lo = split2(v)
    r = jnp.dot(
        jnp.concatenate([hi, lo], 1), jnp.concatenate([w, w], 0), preferred_element_type=F32
    )
    return r[:, :HALF] + r[:, HALF:]


def tile_copies(own, sib, vals, sems, first_sem):
    tiles = own.shape[0]
    copies = []
    for core, src in enumerate((own, sib)):
        for at in range(0, tiles, CHUNK):
            copies.append(
                pltpu.make_async_copy(
                    src.at[pl.ds(at, CHUNK)],
                    vals.at[pl.ds(core * tiles + at, CHUNK)],
                    sems.at[first_sem + len(copies)],
                )
            )
    return copies


def subject_kernel(places, cnt, sub, obj, scale, own, sib, *rest):
    pieces = rest[: len(places)]
    out, raw, parts, vals, sems = rest[len(places) :]
    tiles = own.shape[0]
    rows = []
    for k, (ref, where) in enumerate(zip(pieces, places)):
        n = ref.shape[0] // len(where)
        for j, (z, x, first) in enumerate(where):
            rows.append(
                pltpu.make_async_copy(
                    ref.at[pl.ds(j * n, n)], raw.at[z, x, pl.ds(first, n)], sems.at[ROW_SEM]
                )
            )
    for copy in rows:
        copy.start()
    copies = tile_copies(own, sib, vals, sems, 0)
    for copy in copies:
        copy.start()
    out[...] = jnp.zeros_like(out)
    for copy in rows:
        copy.wait()
    for z in range(NZ):
        for x in range(NX):
            for b in range(4):
                hi, lo = split2(raw[z, x, b * SIDE : (b + 1) * SIDE])
                n = (z * NX + x) * 4 + b
                parts[n, :, :HALF] = hi
                parts[n, :, HALF:] = lo

    def run(base, live):
        def step(g, carry):
            terms = []
            for u in range(GROUP):
                q = base + g * GROUP + u
                terms.append(tile_dot(vals[q], parts[obj[q]]) * scale[pl.ds(q, 1), :])
            for u in range(GROUP):
                out[sub[base + g * GROUP + u]] += terms[u]
            return carry

        lax.fori_loop(0, (live + GROUP - 1) // GROUP, step, 0)

    for k, copy in enumerate(copies):
        copy.wait()
        core, first_tile = divmod(k * CHUNK, tiles)
        run(k * CHUNK, jnp.clip(cnt[core] - first_tile, 0, CHUNK))


def object_kernel(cnt, sub, obj, scale, rows, own, sib, acc, parts, vals, sems):
    tiles = own.shape[0]
    copies = tile_copies(own, sib, vals, sems, 0)
    for copy in copies:
        copy.start()
    acc[...] = jnp.zeros_like(acc)
    for b in range(4):
        hi, lo = split2(rows[b])
        parts[b, :, :HALF] = hi
        parts[b, :, HALF:] = lo

    def run(base, live):
        def step(g, carry):
            terms = []
            for u in range(GROUP):
                q = base + g * GROUP + u
                terms.append(tile_dot(vals[q].T, parts[sub[q]]) * scale[pl.ds(q, 1), :])
            for u in range(GROUP):
                at = pl.multiple_of(obj[base + g * GROUP + u] * SIDE, SIDE)
                acc[pl.ds(at, SIDE), :] += terms[u]
            return carry

        lax.fori_loop(0, (live + GROUP - 1) // GROUP, step, 0)

    for k, copy in enumerate(copies):
        copy.wait()
        core, first_tile = divmod(k * CHUNK, tiles)
        run(k * CHUNK, jnp.clip(cnt[core] - first_tile, 0, CHUNK))


SMEM = pl.BlockSpec(memory_space=pltpu.SMEM)
VMEM = pl.BlockSpec(memory_space=pltpu.VMEM)
ANY = pl.BlockSpec(memory_space=pl.ANY)
PARAMS = pltpu.CompilerParams(vmem_limit_bytes=40 << 20)


def subject_terms(cnt, sub, obj, scale, own, sib, pieces):
    return pl.pallas_call(
        functools.partial(subject_kernel, [where for _, where in pieces]),
        in_specs=[SMEM] * 3 + [VMEM] + [ANY] * (2 + len(pieces)),
        out_specs=VMEM,
        out_shape=jax.ShapeDtypeStruct((4, SIDE, HALF), F32),
        scratch_shapes=[
            pltpu.VMEM((NZ, NX, CHIP_ROWS, HALF), F32),
            pltpu.VMEM((BLOCKS, SIDE, 2 * HALF), BF),
            pltpu.VMEM((2 * own.shape[0], SIDE, SIDE), F32),
            pltpu.SemaphoreType.DMA((ROW_SEM + 1,)),
        ],
        compiler_params=PARAMS,
        name="subject_terms",
    )(cnt, sub, obj, scale, own, sib, *[v for v, _ in pieces])


def object_terms(cnt, sub, obj, scale, rows, own, sib):
    return pl.pallas_call(
        object_kernel,
        in_specs=[SMEM] * 3 + [VMEM] * 2 + [ANY] * 2,
        out_specs=VMEM,
        out_shape=jax.ShapeDtypeStruct((BLOCKS * SIDE, HALF), F32),
        scratch_shapes=[
            pltpu.VMEM((4, SIDE, 2 * HALF), BF),
            pltpu.VMEM((2 * own.shape[0], SIDE, SIDE), F32),
            pltpu.SemaphoreType.DMA((2 * own.shape[0] // CHUNK,)),
        ],
        compiler_params=PARAMS,
        name="object_terms",
    )(cnt, sub, obj, scale, rows, own, sib)


def body(
    tile_values,
    tile_subject,
    tile_object,
    tile_relation,
    tile_day,
    tile_count,
    object_factor,
    relation_factor,
    day_factor,
):
    s = lax.axis_index("subj")
    d = lax.axis_index("day")
    c = s % 2
    here_x = s // 2 % NX
    here_z = s // 8
    own = tile_values[0]
    tiles = own.shape[0]

    meta = jnp.concatenate(
        [
            tile_subject + 2 * c,
            tile_object,
            tile_relation,
            tile_day,
            jnp.broadcast_to(tile_count, (1, tiles)),
        ],
        0,
    )
    unit = to_chip(object_factor, c)
    meta2 = flip(meta, 1)

    unit, meta2, gram = lax.optimization_barrier((unit, meta2, gram_part(object_factor, d)))
    pieces, sib, gram, days = gather_rows(unit, gram, own, d, day_factor)

    sub = jnp.concatenate([meta[0], meta2[0]])
    obj = jnp.concatenate([meta[1], meta2[1]])
    rel = jnp.concatenate([meta[2], meta2[2]])
    day = jnp.concatenate([meta[3], meta2[3]])
    cnt = jnp.concatenate([meta[4, :1], meta2[4, :1]])
    p = obj // 2
    off_z = (p // 8 - here_z) % NZ
    off_x = (p // 2 % NX - here_x) % NX
    slot = ((off_z * NX + off_x) * 2 + p % 2) * 2 + obj % 2
    k = jnp.arange(tiles)
    live = jnp.concatenate([k < cnt[0], k < cnt[1]])
    rel_cols = lax.dynamic_slice_in_dim(relation_factor, c * HALF, HALF, 1)
    day_cols = lax.dynamic_slice_in_dim(day_factor, c * HALF, HALF, 1)
    rel_pick = (rel[:, None] == jnp.arange(relation_factor.shape[0])[None, :]).astype(F32)
    day_pick = (day[:, None] == jnp.arange(day_factor.shape[0])[None, :]).astype(F32)
    scale = jnp.dot(rel_pick, rel_cols, precision=HIGH) * jnp.dot(
        day_pick, day_cols, precision=HIGH
    )
    scale = scale * live[:, None].astype(F32)

    gram_rest = jnp.dot(relation_factor.T, relation_factor, precision=HIGH) * jnp.dot(
        days.T, days, precision=HIGH
    )
    gram_first = gram * gram_rest

    part = subject_terms(cnt, sub, slot, scale, own, sib, pieces)
    part, gram_first = lax.optimization_barrier((part, gram_first))
    total = day_sum(to_core(part.reshape(CHIP_ROWS, HALF), c))
    inv_first = inverse_factor(gram_first)
    raw = solve_rows(total, inv_first)
    lifted = raw * LIFT
    rows = to_chip(lifted, c).reshape(4, SIDE, HALF)

    gram = gram_part(lifted, d)
    gram = gram + flip(gram, 1)
    rows, gram = lax.optimization_barrier((rows, gram))
    moved = [flip(gram, mask) for mask in (2, 4, 6)]
    back = object_terms(cnt, sub, slot, scale, rows, own, sib)
    back, gram, moved = lax.optimization_barrier((back, gram, moved))
    back = back.reshape(NZ, NX, CHIP_ROWS, HALF)
    rows, gram = scatter_rows(back, (gram + moved[0]) + (moved[1] + moved[2]), d)
    gram_second = gram * gram_rest
    rows, gram_second = lax.optimization_barrier((rows, gram_second))
    total = day_sum(to_core(rows, c))
    inv_second = inverse_factor(gram_second)
    raw_b = solve_rows(total, inv_second)

    tops = jnp.stack([jnp.max(jnp.abs(raw), axis=0), jnp.max(jnp.abs(raw_b), axis=0)])
    spread = jnp.broadcast_to(tops[None], (64,) + tops.shape)
    tops = jnp.max(lax.all_to_all(spread, "subj", 0, 0, tiled=True), axis=0)
    fall = tops[0] + EPS
    grown = fall * LIFT
    return (raw / fall, raw_b * (grown / (tops[1] * grown + EPS)))


def solution(mesh):
    return jax.shard_map(
        body,
        mesh=mesh,
        in_specs=(
            P("day", "subj", None, None),
            P("day", "subj"),
            P("day", "subj"),
            P("day", "subj"),
            P("day", "subj"),
            P("day", "subj"),
            P("subj", None),
            P(),
            P("day", None),
        ),
        out_specs=(P("subj", None), P("subj", None)),
        check_vma=False,
    )
```

```python
import functools

import jax
import jax.numpy as jnp
from jax import lax
from jax.experimental import pallas as pl
from jax.experimental.pallas import tpu as pltpu
from jax.sharding import PartitionSpec as P

F32 = jnp.float32
BF = jnp.bfloat16
HIGH = lax.Precision.HIGHEST
EPS = 1e-06
LIFT = 65536.0

NZ, NX = 8, 4
N_DAY = 4
SIDE = 128
HALF = 128
CHIP_ROWS = 512
SPLIT_X = 224
SPLIT_Z = CHIP_ROWS - SPLIT_X
BLOCKS = NZ * NX * 4
STRIP = 16
PANEL = 64
GROUP = 12
CHUNK = 48
ROW_SEM = 4


def pairs_z(k):
    return [(s, ((s // 8 + k) % NZ) * 8 + s % 8) for s in range(64)]


def pairs_x(k):
    return [(s, (s // 8) * 8 + ((s // 2 % 4 + k) % NX) * 2 + s % 2) for s in range(64)]


def flip(x, mask):
    return lax.ppermute(x, "subj", [(s, s ^ mask) for s in range(64)])


def flip_day(x, mask):
    return lax.ppermute(x, "day", [(s, s ^ mask) for s in range(N_DAY)])


def step(moves, *keep):
    got = [
        lax.ppermute(v, "subj", pairs) if axis == "subj" else flip_day(v, pairs)
        for v, axis, pairs in moves
    ]
    return lax.optimization_barrier((got, keep))


def xup(v):
    return (v, "subj", pairs_x(1))


def xdown(v):
    return (v, "subj", pairs_x(-1))


def zup(v):
    return (v, "subj", pairs_z(1))


def zdown(v):
    return (v, "subj", pairs_z(-1))


def mate(v, mask):
    return (v, "subj", [(s, s ^ mask) for s in range(64)])


def day_mate(v, mask):
    return (v, "day", mask)


def cut(v):
    h = v.shape[0] // 2
    return v[:h], v[h:]


def stack(*parts):
    return jnp.concatenate(parts, 0)


def pack(g):
    return stack(g[:, :HALF], g[:, HALF:])


def unpack(p):
    n = p.shape[0] // 2
    return jnp.concatenate([p[:n], p[n:]], 1)


def gather_rows(unit, gram, own, d, days):
    a, b = unit[:SPLIT_X], unit[SPLIT_X:]
    na, nb = SPLIT_X, SPLIT_Z
    m = stack(b, gram)
    (au, ad, bu1, bd1), (a,) = step([xup(a), xdown(a), zup(m), zdown(m)], a)
    (at, ab, bu2, bd2), () = step([xup(cut(au)[0]), xdown(cut(ad)[1]), zup(bu1), zdown(bd1)])
    (bu3, bd3), () = step([zup(bu2), zdown(bd2)])
    h = nb // 2
    (bt, bb), () = step([zup(stack(bu3[:h], bu3[nb:])), zdown(bd3[h:nb])])
    gram = gram + bu1[nb:] + bd1[nb:] + bu2[nb:] + bd2[nb:] + bu3[nb:] + bd3[nb:] + bt[h:]
    a = stack(a, ad, at, ab, au)
    low = stack(b, bd1[:nb], bd2[:nb], bd3[:nb], gram)
    high = stack(bt[:h], bb, bu3[:nb], bu2[:nb], bu1[:nb])
    a, low, high, gram = lax.optimization_barrier((a, low, high, gram))
    (au1, ad1, lu, ld), (a, low, high, own) = step(
        [zup(a), zdown(a), xup(low), xdown(low)], a, low, high, own
    )
    far = lu[4 * nb :]
    gram = gram + far + ld[4 * nb :]
    (au2, ad2, hu, hd, sib), (lu, gram) = step(
        [zup(au1), zdown(ad1), xup(stack(high, far)), xdown(high), mate(own, 1)], lu, gram
    )
    gram = gram + hu[4 * nb :]
    (au3, ad3, lf, hf, g), (gram,) = step(
        [zup(au2), zdown(ad2), xup(lu), xdown(hd), mate(gram, 1)], gram
    )
    gram = unpack(gram + g)
    n = gram.shape[0]
    (at, ab, g), (gram,) = step(
        [zup(cut(au3)[0]), zdown(cut(ad3)[1]), day_mate(stack(gram, days), 1)], gram
    )
    gram = day_join(gram, g[:n], d % 2)
    days = day_join(days, g[n:], d % 2)
    g = flip_day(stack(gram, days), 2)
    gram = day_join(gram, g[: 2 * n], d // 2)
    days = day_join(days, g[2 * n :], d // 2)
    pieces = []
    for z, v in ((0, a), (1, ad1), (2, ad2), (3, ad3), (5, au3), (6, au2), (7, au1)):
        pieces.append((v, [(z, x, 0, x * na, na) for x in range(NX)]))
    for v, first in ((at, 0), (ab, 2)):
        pieces.append((v, [(4, first + x, 0, x * na, na) for x in range(2)]))
    for x, v, first in (
        (0, low, 0), (3, lu, 0), (1, ld, 0), (2, lf, 0),
        (0, high, 4), (3, hu, 4), (1, hd, 4), (2, hf, 4),
    ):
        pieces.append((v, [(first + z, x, na, z * nb, nb) for z in range(4)]))
    return pieces, sib, gram, days


def scatter_rows(back, gram, d):
    def to_z(z):
        return back[z, :, :SPLIT_X].reshape(NX * SPLIT_X, HALF)

    def to_x(x, first):
        return back[first : first + 4, x, SPLIT_X:].reshape(4 * SPLIT_Z, HALF)

    n = NX * SPLIT_X
    h = n // 2
    far_top, far_low = cut(to_z(4))
    (u, v, lu, hd), (gram, late_up, late_down) = step(
        [zup(stack(far_top, gram)), zdown(stack(far_low, gram)), xup(to_x(2, 0)), xdown(to_x(2, 4))],
        gram, to_x(1, 4), to_x(3, 0),
    )
    gram = gram + u[h:] + v[h:]
    p, q = to_z(3), to_z(5)
    p = stack(p[:h] + u[:h], p[h:], u[h:])
    q = stack(q[:h], q[h:] + v[:h], v[h:])
    (u, v, lu, hd), (gram, late_up, late_down) = step(
        [zup(p), zdown(q), xup(to_x(1, 0) + lu), xdown(to_x(3, 4) + hd)],
        gram, late_up, late_down,
    )
    gram = gram + u[n:] + v[n:]
    p = stack(to_z(2) + u[:n], u[n:])
    q = stack(to_z(6) + v[:n], v[n:])
    (u, v, hu, ld), (gram, lu, hd) = step(
        [zup(p), zdown(q), xup(late_up), xdown(late_down)], gram, lu, hd
    )
    gram = gram + u[n:] + v[n:]
    low = to_x(0, 0) + lu + ld
    high = to_x(0, 4) + hu + hd
    b = [low[k * SPLIT_Z : (k + 1) * SPLIT_Z] for k in range(4)]
    b += [high[k * SPLIT_Z : (k + 1) * SPLIT_Z] for k in range(4)]
    p = stack(to_z(1) + u[:n], u[n:])
    q = to_z(7) + v[:n]
    (u, v, bu, bv), (gram, b) = step(
        [zup(p), zdown(q), zup(cut(b[4])[0]), zdown(cut(b[4])[1])], gram, b
    )
    gram = unpack(gram + u[n:])
    a = to_z(0) + u[:n] + v
    a = [a[k * SPLIT_X : (k + 1) * SPLIT_X] for k in range(NX)]
    p = stack(cut(b[3])[0] + bu, cut(b[3])[1])
    q = stack(cut(b[5])[0], cut(b[5])[1] + bv)
    (bu, bv, u, v, g), (gram, a, b) = step(
        [zup(p), zdown(q), xup(cut(a[2])[0]), xdown(cut(a[2])[1]), day_mate(gram, 1)], gram, a, b
    )
    gram = day_join(gram, g, d % 2)
    p = stack(cut(a[1])[0] + u, cut(a[1])[1])
    q = stack(cut(a[3])[0], cut(a[3])[1] + v)
    (bu, bv, u, v, g), (gram, a, b) = step(
        [zup(b[2] + bu), zdown(b[6] + bv), xup(p), xdown(q), day_mate(gram, 2)], gram, a, b
    )
    gram = day_join(gram, g, d // 2)
    a = a[0] + u + v
    (bu, bv), (a, b) = step([zup(b[1] + bu), zdown(b[7] + bv)], a, b)
    return stack(a, b[0] + bu + bv), gram


def day_join(mine, moved, late):
    return jnp.where(
        late == 1, jnp.concatenate([moved, mine], 0), jnp.concatenate([mine, moved], 0)
    )


def day_sum(x):
    return (x + flip_day(x, 1)) + (flip_day(x, 2) + flip_day(x, 3))


def core_order(c, mine, other, axis):
    return jnp.where(
        c == 0,
        jnp.concatenate([mine, other], axis),
        jnp.concatenate([other, mine], axis),
    )


def to_chip(m, c):
    mine = lax.dynamic_slice_in_dim(m, c * HALF, HALF, 1)
    send = lax.dynamic_slice_in_dim(m, (1 - c) * HALF, HALF, 1)
    return core_order(c, mine, flip(send, 1), 0)


def to_core(u, c):
    rows = CHIP_ROWS // 2
    mine = lax.dynamic_slice_in_dim(u, c * rows, rows, 0)
    send = lax.dynamic_slice_in_dim(u, (1 - c) * rows, rows, 0)
    return core_order(c, mine, flip(send, 1), 1)


def gram_part(m, d):
    quarter = m.shape[1] // N_DAY
    cols = lax.dynamic_slice_in_dim(m, d * quarter, quarter, 1)
    return jnp.dot(cols.T, m, precision=HIGH)


def exact_dot(a, b):
    return jnp.dot(a, b, precision=HIGH, preferred_element_type=F32)


def unit_matrix(n):
    i = lax.broadcasted_iota(jnp.int32, (n, n), 0)
    return (i == lax.broadcasted_iota(jnp.int32, (n, n), 1)).astype(F32)


def block_inverse(block):
    n = block.shape[0]
    wide = jnp.concatenate([block, unit_matrix(n)], 1)
    place = lax.broadcasted_iota(jnp.int32, wide.shape, 0)
    for p in range(0, n, STRIP):
        cols = [jnp.broadcast_to(wide[:, p + j : p + j + 1], wide.shape) for j in range(STRIP)]
        for j in range(STRIP):
            k = p + j
            pivot = cols[j][k : k + 1, :]
            r = lax.rsqrt(pivot)
            r = r * (1.5 - 0.5 * (pivot * r) * r)
            col = cols[j] * r
            row = wide[k : k + 1, :] * r
            below = jnp.where(place > k, col, 0.0)
            wide = jnp.where(place == k, row, wide - below * row)
            for t in range(j + 1, STRIP):
                cols[t] = cols[t] - below * col[p + t : p + t + 1, :]
    return wide[:, n:]


def factor_kernel(gram, out, work):
    n = gram.shape[0]
    work[...] = gram[...]
    out[...] = unit_matrix(n)
    for b in range(0, n, PANEL):
        e = b + PANEL
        inv = block_inverse(work[b:e, b:e])
        used = -(-e // 128) * 128
        top = exact_dot(inv, out[b:e, :used])
        out[b:e, :used] = top
        if e < n:
            panel = lax.dot_general(
                work[e:n, b:e], inv, (((1,), (1,)), ((), ())), precision=HIGH,
                preferred_element_type=F32,
            )
            work[e:n, e:n] -= lax.dot_general(
                panel, panel, (((1,), (1,)), ((), ())), precision=HIGH,
                preferred_element_type=F32,
            )
            out[e:n, :used] -= exact_dot(panel, top)


def inverse_factor(gram):
    return pl.pallas_call(
        factor_kernel,
        out_shape=jax.ShapeDtypeStruct(gram.shape, F32),
        scratch_shapes=[pltpu.VMEM(gram.shape, F32)],
        name="inverse_factor",
    )(gram)


def solve_rows(total, inv):
    y = jnp.dot(total, inv.T, precision=HIGH)
    return jnp.dot(y, inv, precision=HIGH)


def split2(x):
    hi = x.astype(BF)
    lo = (x - hi.astype(F32)).astype(BF)
    return hi, lo


def tile_dot(v, w):
    hi, lo = split2(v)
    r = jnp.dot(
        jnp.concatenate([hi, lo], 1), jnp.concatenate([w, w], 0), preferred_element_type=F32
    )
    return r[:, :HALF] + r[:, HALF:]


def tile_copies(own, sib, vals, sems, first_sem):
    tiles = own.shape[0]
    copies = []
    for core, src in enumerate((own, sib)):
        for at in range(0, tiles, CHUNK):
            copies.append(
                pltpu.make_async_copy(
                    src.at[pl.ds(at, CHUNK)],
                    vals.at[pl.ds(core * tiles + at, CHUNK)],
                    sems.at[first_sem + len(copies)],
                )
            )
    return copies


def subject_kernel(places, cnt, sub, obj, scale, own, sib, *rest):
    pieces = rest[: len(places)]
    out, raw, parts, vals, sems = rest[len(places) :]
    tiles = own.shape[0]
    rows = [
        pltpu.make_async_copy(
            ref.at[pl.ds(here, n)], raw.at[z, x, pl.ds(there, n)], sems.at[ROW_SEM]
        )
        for ref, where in zip(pieces, places)
        for z, x, there, here, n in where
    ]
    for copy in rows:
        copy.start()
    copies = tile_copies(own, sib, vals, sems, 0)
    for copy in copies:
        copy.start()
    out[...] = jnp.zeros_like(out)
    for copy in rows:
        copy.wait()
    for z in range(NZ):
        for x in range(NX):
            for b in range(4):
                hi, lo = split2(raw[z, x, b * SIDE : (b + 1) * SIDE])
                n = (z * NX + x) * 4 + b
                parts[n, :, :HALF] = hi
                parts[n, :, HALF:] = lo

    def run(base, live):
        def step(g, carry):
            terms = []
            for u in range(GROUP):
                q = base + g * GROUP + u
                terms.append(tile_dot(vals[q], parts[obj[q]]) * scale[pl.ds(q, 1), :])
            for u in range(GROUP):
                out[sub[base + g * GROUP + u]] += terms[u]
            return carry

        lax.fori_loop(0, (live + GROUP - 1) // GROUP, step, 0)

    for k, copy in enumerate(copies):
        copy.wait()
        core, first_tile = divmod(k * CHUNK, tiles)
        run(k * CHUNK, jnp.clip(cnt[core] - first_tile, 0, CHUNK))


def object_kernel(cnt, sub, obj, scale, rows, own, sib, acc, parts, vals, sems):
    tiles = own.shape[0]
    copies = tile_copies(own, sib, vals, sems, 0)
    for copy in copies:
        copy.start()
    acc[...] = jnp.zeros_like(acc)
    for b in range(4):
        hi, lo = split2(rows[b])
        parts[b, :, :HALF] = hi
        parts[b, :, HALF:] = lo

    def run(base, live):
        def step(g, carry):
            terms = []
            for u in range(GROUP):
                q = base + g * GROUP + u
                terms.append(tile_dot(vals[q].T, parts[sub[q]]) * scale[pl.ds(q, 1), :])
            for u in range(GROUP):
                at = pl.multiple_of(obj[base + g * GROUP + u] * SIDE, SIDE)
                acc[pl.ds(at, SIDE), :] += terms[u]
            return carry

        lax.fori_loop(0, (live + GROUP - 1) // GROUP, step, 0)

    for k, copy in enumerate(copies):
        copy.wait()
        core, first_tile = divmod(k * CHUNK, tiles)
        run(k * CHUNK, jnp.clip(cnt[core] - first_tile, 0, CHUNK))


SMEM = pl.BlockSpec(memory_space=pltpu.SMEM)
VMEM = pl.BlockSpec(memory_space=pltpu.VMEM)
HBM = pl.BlockSpec(memory_space=pltpu.HBM)
PARAMS = pltpu.CompilerParams(vmem_limit_bytes=32 << 20)


def subject_terms(cnt, sub, obj, scale, own, sib, pieces):
    return pl.pallas_call(
        functools.partial(subject_kernel, [where for _, where in pieces]),
        in_specs=[SMEM] * 3 + [VMEM] + [HBM] * (2 + len(pieces)),
        out_specs=VMEM,
        out_shape=jax.ShapeDtypeStruct((4, SIDE, HALF), F32),
        scratch_shapes=[
            pltpu.VMEM((NZ, NX, CHIP_ROWS, HALF), F32),
            pltpu.VMEM((BLOCKS, SIDE, 2 * HALF), BF),
            pltpu.VMEM((2 * own.shape[0], SIDE, SIDE), F32),
            pltpu.SemaphoreType.DMA((ROW_SEM + 1,)),
        ],
        compiler_params=PARAMS,
        name="subject_terms",
    )(cnt, sub, obj, scale, own, sib, *[v for v, _ in pieces])


def object_terms(cnt, sub, obj, scale, rows, own, sib):
    return pl.pallas_call(
        object_kernel,
        in_specs=[SMEM] * 3 + [VMEM] * 2 + [HBM] * 2,
        out_specs=VMEM,
        out_shape=jax.ShapeDtypeStruct((BLOCKS * SIDE, HALF), F32),
        scratch_shapes=[
            pltpu.VMEM((4, SIDE, 2 * HALF), BF),
            pltpu.VMEM((2 * own.shape[0], SIDE, SIDE), F32),
            pltpu.SemaphoreType.DMA((2 * own.shape[0] // CHUNK,)),
        ],
        compiler_params=PARAMS,
        name="object_terms",
    )(cnt, sub, obj, scale, rows, own, sib)


def body(
    tile_values,
    tile_subject,
    tile_object,
    tile_relation,
    tile_day,
    tile_count,
    object_factor,
    relation_factor,
    day_factor,
):
    s = lax.axis_index("subj")
    d = lax.axis_index("day")
    c = s % 2
    here_x = s // 2 % NX
    here_z = s // 8
    own = tile_values[0]
    tiles = own.shape[0]

    meta = jnp.concatenate(
        [
            tile_subject + 2 * c,
            tile_object,
            tile_relation,
            tile_day,
            jnp.broadcast_to(tile_count, (1, tiles)),
        ],
        0,
    )
    unit = to_chip(object_factor, c)
    meta2 = flip(meta, 1)

    unit, meta2, gram = lax.optimization_barrier(
        (unit, meta2, pack(gram_part(object_factor, d)))
    )
    pieces, sib, gram, days = gather_rows(unit, gram, own, d, day_factor)

    sub = jnp.concatenate([meta[0], meta2[0]])
    obj = jnp.concatenate([meta[1], meta2[1]])
    rel = jnp.concatenate([meta[2], meta2[2]])
    day = jnp.concatenate([meta[3], meta2[3]])
    cnt = jnp.concatenate([meta[4, :1], meta2[4, :1]])
    p = obj // 2
    off_z = (p // 8 - here_z) % NZ
    off_x = (p // 2 % NX - here_x) % NX
    slot = ((off_z * NX + off_x) * 2 + p % 2) * 2 + obj % 2
    k = jnp.arange(tiles)
    live = jnp.concatenate([k < cnt[0], k < cnt[1]])
    rel_cols = lax.dynamic_slice_in_dim(relation_factor, c * HALF, HALF, 1)
    day_cols = lax.dynamic_slice_in_dim(day_factor, c * HALF, HALF, 1)
    rel_pick = (rel[:, None] == jnp.arange(relation_factor.shape[0])[None, :]).astype(F32)
    day_pick = (day[:, None] == jnp.arange(day_factor.shape[0])[None, :]).astype(F32)
    scale = jnp.dot(rel_pick, rel_cols, precision=HIGH) * jnp.dot(
        day_pick, day_cols, precision=HIGH
    )
    scale = scale * live[:, None].astype(F32)

    gram_rest = jnp.dot(relation_factor.T, relation_factor, precision=HIGH) * jnp.dot(
        days.T, days, precision=HIGH
    )
    gram_first = gram * gram_rest

    part = subject_terms(cnt, sub, slot, scale, own, sib, pieces)
    part, gram_first = lax.optimization_barrier((part, gram_first))
    total = day_sum(to_core(part.reshape(CHIP_ROWS, HALF), c))
    inv_first = inverse_factor(gram_first)
    raw = solve_rows(total, inv_first)
    lifted = raw * LIFT
    rows = to_chip(lifted, c).reshape(4, SIDE, HALF)

    gram = gram_part(lifted, d)
    gram = gram + flip(gram, 1)
    rows, gram = lax.optimization_barrier((rows, gram))
    moved = [flip(gram, mask) for mask in (2, 4, 6)]
    back = object_terms(cnt, sub, slot, scale, rows, own, sib)
    back, gram, moved = lax.optimization_barrier((back, gram, moved))
    back = back.reshape(NZ, NX, CHIP_ROWS, HALF)
    rows, gram = scatter_rows(back, pack((gram + moved[0]) + (moved[1] + moved[2])), d)
    gram_second = gram * gram_rest
    rows, gram_second = lax.optimization_barrier((rows, gram_second))
    total = day_sum(to_core(rows, c))
    inv_second = inverse_factor(gram_second)
    raw_b = solve_rows(total, inv_second)

    tops = jnp.stack([jnp.max(jnp.abs(raw), axis=0), jnp.max(jnp.abs(raw_b), axis=0)])
    spread = jnp.broadcast_to(tops[None], (64,) + tops.shape)
    tops = jnp.max(lax.all_to_all(spread, "subj", 0, 0, tiled=True), axis=0)
    fall = tops[0] + EPS
    grown = fall * LIFT
    return (raw / fall, raw_b * (grown / (tops[1] * grown + EPS)))


def solution(mesh):
    return jax.shard_map(
        body,
        mesh=mesh,
        in_specs=(
            P("day", "subj", None, None),
            P("day", "subj"),
            P("day", "subj"),
            P("day", "subj"),
            P("day", "subj"),
            P("day", "subj"),
            P("subj", None),
            P(),
            P("day", None),
        ),
        out_specs=(P("subj", None), P("subj", None)),
        check_vma=False,
    )
```

```python
import functools

import jax
import jax.numpy as jnp
from jax import lax
from jax.experimental import pallas as pl
from jax.experimental.pallas import tpu as pltpu
from jax.sharding import PartitionSpec as P

F32 = jnp.float32
BF = jnp.bfloat16
HIGH = lax.Precision.HIGHEST
EPS = 1e-06
LIFT = 65536.0

NZ, NX = 8, 4
N_DAY = 4
SIDE = 128
HALF = 128
CHIP_ROWS = 512
SPLIT_X = 224
SPLIT_Z = CHIP_ROWS - SPLIT_X
BLOCKS = NZ * NX * 4
STRIP = 16
PANEL = 64
GROUP = 12
CHUNK = 48
ROW_SEM = 4


def pairs_z(k):
    return [(s, ((s // 8 + k) % NZ) * 8 + s % 8) for s in range(64)]


def pairs_x(k):
    return [(s, (s // 8) * 8 + ((s // 2 % 4 + k) % NX) * 2 + s % 2) for s in range(64)]


def flip(x, mask):
    return lax.ppermute(x, "subj", [(s, s ^ mask) for s in range(64)])


def flip_day(x, mask):
    return lax.ppermute(x, "day", [(s, s ^ mask) for s in range(N_DAY)])


def step(moves, *keep):
    got = [
        lax.ppermute(v, "subj", pairs) if axis == "subj" else flip_day(v, pairs)
        for v, axis, pairs in moves
    ]
    return lax.optimization_barrier((got, keep))


def xup(v):
    return (v, "subj", pairs_x(1))


def xdown(v):
    return (v, "subj", pairs_x(-1))


def zup(v):
    return (v, "subj", pairs_z(1))


def zdown(v):
    return (v, "subj", pairs_z(-1))


def mate(v, mask):
    return (v, "subj", [(s, s ^ mask) for s in range(64)])


def day_mate(v, mask):
    return (v, "day", mask)


def cut(v):
    h = v.shape[0] // 2
    return v[:h], v[h:]


def stack(*parts):
    return jnp.concatenate(parts, 0)


def pack(g):
    return stack(g[:, :HALF], g[:, HALF:])


def unpack(p):
    n = p.shape[0] // 2
    return jnp.concatenate([p[:n], p[n:]], 1)


def gather_rows(unit, gram, own, d, days):
    a, b = unit[:SPLIT_X], unit[SPLIT_X:]
    na, nb = SPLIT_X, SPLIT_Z
    m = stack(b, gram)
    (au, ad, bu1, bd1), (a,) = step([xup(a), xdown(a), zup(m), zdown(m)], a)
    (at, ab, bu2, bd2), () = step([xup(cut(au)[0]), xdown(cut(ad)[1]), zup(bu1), zdown(bd1)])
    (bu3, bd3), () = step([zup(bu2), zdown(bd2)])
    h = nb // 2
    (bt, bb), () = step([zup(stack(bu3[:h], bu3[nb:])), zdown(bd3[h:nb])])
    gram = gram + bu1[nb:] + bd1[nb:] + bu2[nb:] + bd2[nb:] + bu3[nb:] + bd3[nb:] + bt[h:]
    a = stack(a, ad, at, ab, au)
    low = stack(b, bd1[:nb], bd2[:nb], bd3[:nb], gram)
    high = stack(bt[:h], bb, bu3[:nb], bu2[:nb], bu1[:nb], gram)
    a, low, high, gram = lax.optimization_barrier((a, low, high, gram))
    (au1, ad1, lu, ld), (a, low, high, own) = step(
        [zup(a), zdown(a), xup(low), xdown(low)], a, low, high, own
    )
    far = lu[4 * nb :]
    gram = gram + far + ld[4 * nb :]
    high = lax.dynamic_update_slice(high, far, (4 * nb, 0))
    (au2, ad2, hu, hd, sib), (lu, gram) = step(
        [zup(au1), zdown(ad1), xup(high), xdown(high), mate(own, 1)], lu, gram
    )
    gram = unpack(gram + hu[4 * nb :])
    n = gram.shape[0]
    (au3, ad3, lf, hf, g), (gram,) = step(
        [zup(au2), zdown(ad2), xup(lu), xdown(hd), day_mate(stack(gram, days), 1)], gram
    )
    gram = day_join(gram, g[:n], d % 2)
    days = day_join(days, g[n:], d % 2)
    (at, ab, g), (gram, days) = step(
        [zup(cut(au3)[0]), zdown(cut(ad3)[1]), day_mate(stack(gram, days), 2)], gram, days
    )
    gram = day_join(gram, g[: 2 * n], d // 2)
    days = day_join(days, g[2 * n :], d // 2)
    pieces = []
    for z, v in ((0, a), (1, ad1), (2, ad2), (3, ad3), (5, au3), (6, au2), (7, au1)):
        pieces.append((v, [(z, x, 0, x * na, na) for x in range(NX)]))
    for v, first in ((at, 0), (ab, 2)):
        pieces.append((v, [(4, first + x, 0, x * na, na) for x in range(2)]))
    for x, v, first in (
        (0, low, 0), (3, lu, 0), (1, ld, 0), (2, lf, 0),
        (0, high, 4), (3, hu, 4), (1, hd, 4), (2, hf, 4),
    ):
        pieces.append((v, [(first + z, x, na, z * nb, nb) for z in range(4)]))
    return pieces, sib, gram, days


def scatter_rows(back, gram, d):
    def to_z(z):
        return back[z, :, :SPLIT_X].reshape(NX * SPLIT_X, HALF)

    def to_x(x, first):
        return back[first : first + 4, x, SPLIT_X:].reshape(4 * SPLIT_Z, HALF)

    n, nb = NX * SPLIT_X, SPLIT_Z
    h, w = n // 2, 4 * nb
    far_top, far_low = cut(to_z(4))
    (u, v, lu, hd), (gram, late_up, late_down) = step(
        [
            zup(far_top), zdown(far_low),
            xup(stack(to_x(2, 0), gram)), xdown(stack(to_x(2, 4), gram)),
        ],
        gram, to_x(1, 4), to_x(3, 0),
    )
    gram = gram + lu[w:] + hd[w:]
    p, q = to_z(3), to_z(5)
    p = stack(p[:h] + u, p[h:])
    q = stack(q[:h], q[h:] + v)
    (u, v, lu, hd), (gram, late_up, late_down) = step(
        [zup(p), zdown(q), xup(stack(to_x(1, 0) + lu[:w], lu[w:])), xdown(to_x(3, 4) + hd[:w])],
        gram, late_up, late_down,
    )
    gram = gram + lu[w:]
    (u, v, hu, ld), (gram, lu, hd) = step(
        [
            zup(stack(to_z(2) + u, gram)), zdown(stack(to_z(6) + v, gram)),
            xup(late_up), xdown(late_down),
        ],
        gram, lu, hd,
    )
    gram = gram + u[n:] + v[n:]
    low = to_x(0, 0) + lu[:w] + ld
    high = to_x(0, 4) + hu + hd
    b = [low[k * nb : (k + 1) * nb] for k in range(4)]
    b += [high[k * nb : (k + 1) * nb] for k in range(4)]
    p = stack(to_z(1) + u[:n], u[n:])
    q = stack(to_z(7) + v[:n], v[n:])
    (u, v, bu, bv), (gram, b) = step(
        [zup(p), zdown(q), zup(cut(b[4])[0]), zdown(cut(b[4])[1])], gram, b
    )
    gram = gram + u[n:] + v[n:]
    a = to_z(0) + u[:n] + v[:n]
    a = [a[k * SPLIT_X : (k + 1) * SPLIT_X] for k in range(NX)]
    p = stack(cut(b[3])[0] + bu, cut(b[3])[1], u[n:])
    q = stack(cut(b[5])[0], cut(b[5])[1] + bv, v[n:])
    (bu, bv, u, v), (gram, a, b) = step(
        [zup(p), zdown(q), xup(cut(a[2])[0]), xdown(cut(a[2])[1])], gram, a, b
    )
    gram = gram + bu[nb:] + bv[nb:]
    p = stack(cut(a[1])[0] + u, cut(a[1])[1])
    q = stack(cut(a[3])[0], cut(a[3])[1] + v)
    (bu, bv, u, v), (gram, a, b) = step(
        [zup(stack(b[2] + bu[:nb], bu[nb:])), zdown(b[6] + bv[:nb]), xup(p), xdown(q)], gram, a, b
    )
    gram = unpack(gram + bu[nb:])
    a = a[0] + u + v
    (bu, bv, g), (gram, a, b) = step(
        [zup(b[1] + bu[:nb]), zdown(b[7] + bv), day_mate(gram, 1)], gram, a, b
    )
    gram = day_join(gram, g, d % 2)
    gram = day_join(gram, flip_day(gram, 2), d // 2)
    return stack(a, b[0] + bu + bv), gram


def day_join(mine, moved, late):
    return jnp.where(
        late == 1, jnp.concatenate([moved, mine], 0), jnp.concatenate([mine, moved], 0)
    )


def day_sum(x):
    return (x + flip_day(x, 1)) + (flip_day(x, 2) + flip_day(x, 3))


def core_order(c, mine, other, axis):
    return jnp.where(
        c == 0,
        jnp.concatenate([mine, other], axis),
        jnp.concatenate([other, mine], axis),
    )


def to_chip(m, c):
    mine = lax.dynamic_slice_in_dim(m, c * HALF, HALF, 1)
    send = lax.dynamic_slice_in_dim(m, (1 - c) * HALF, HALF, 1)
    return core_order(c, mine, flip(send, 1), 0)


def to_core(u, c):
    rows = CHIP_ROWS // 2
    mine = lax.dynamic_slice_in_dim(u, c * rows, rows, 0)
    send = lax.dynamic_slice_in_dim(u, (1 - c) * rows, rows, 0)
    return core_order(c, mine, flip(send, 1), 1)


def gram_part(m, d):
    quarter = m.shape[1] // N_DAY
    cols = lax.dynamic_slice_in_dim(m, d * quarter, quarter, 1)
    return jnp.dot(cols.T, m, precision=HIGH)


def exact_dot(a, b):
    return jnp.dot(a, b, precision=HIGH, preferred_element_type=F32)


def unit_matrix(n):
    i = lax.broadcasted_iota(jnp.int32, (n, n), 0)
    return (i == lax.broadcasted_iota(jnp.int32, (n, n), 1)).astype(F32)


def block_inverse(block):
    n = block.shape[0]
    wide = jnp.concatenate([block, unit_matrix(n)], 1)
    place = lax.broadcasted_iota(jnp.int32, wide.shape, 0)
    for p in range(0, n, STRIP):
        cols = [jnp.broadcast_to(wide[:, p + j : p + j + 1], wide.shape) for j in range(STRIP)]
        for j in range(STRIP):
            k = p + j
            pivot = cols[j][k : k + 1, :]
            r = lax.rsqrt(pivot)
            r = r * (1.5 - 0.5 * (pivot * r) * r)
            col = cols[j] * r
            row = wide[k : k + 1, :] * r
            below = jnp.where(place > k, col, 0.0)
            wide = jnp.where(place == k, row, wide - below * row)
            for t in range(j + 1, STRIP):
                cols[t] = cols[t] - below * col[p + t : p + t + 1, :]
    return wide[:, n:]


def factor_kernel(gram, out, work):
    n = gram.shape[0]
    work[...] = gram[...]
    out[...] = unit_matrix(n)
    for b in range(0, n, PANEL):
        e = b + PANEL
        inv = block_inverse(work[b:e, b:e])
        used = -(-e // 128) * 128
        top = exact_dot(inv, out[b:e, :used])
        out[b:e, :used] = top
        if e < n:
            panel = lax.dot_general(
                work[e:n, b:e], inv, (((1,), (1,)), ((), ())), precision=HIGH,
                preferred_element_type=F32,
            )
            work[e:n, e:n] -= lax.dot_general(
                panel, panel, (((1,), (1,)), ((), ())), precision=HIGH,
                preferred_element_type=F32,
            )
            out[e:n, :used] -= exact_dot(panel, top)


def inverse_factor(gram):
    return pl.pallas_call(
        factor_kernel,
        out_shape=jax.ShapeDtypeStruct(gram.shape, F32),
        scratch_shapes=[pltpu.VMEM(gram.shape, F32)],
        name="inverse_factor",
    )(gram)


def solve_rows(total, inv):
    y = jnp.dot(total, inv.T, precision=HIGH)
    return jnp.dot(y, inv, precision=HIGH)


def split2(x):
    hi = x.astype(BF)
    lo = (x - hi.astype(F32)).astype(BF)
    return hi, lo


def tile_dot(v, w):
    hi, lo = split2(v)
    r = jnp.dot(
        jnp.concatenate([hi, lo], 1), jnp.concatenate([w, w], 0), preferred_element_type=F32
    )
    return r[:, :HALF] + r[:, HALF:]


def tile_copies(own, sib, vals, sems, first_sem):
    tiles = own.shape[0]
    copies = []
    for core, src in enumerate((own, sib)):
        for at in range(0, tiles, CHUNK):
            copies.append(
                pltpu.make_async_copy(
                    src.at[pl.ds(at, CHUNK)],
                    vals.at[pl.ds(core * tiles + at, CHUNK)],
                    sems.at[first_sem + len(copies)],
                )
            )
    return copies


def subject_kernel(places, cnt, sub, obj, scale, own, sib, *rest):
    pieces = rest[: len(places)]
    out, raw, parts, vals, sems = rest[len(places) :]
    tiles = own.shape[0]
    rows = [
        pltpu.make_async_copy(
            ref.at[pl.ds(here, n)], raw.at[z, x, pl.ds(there, n)], sems.at[ROW_SEM]
        )
        for ref, where in zip(pieces, places)
        for z, x, there, here, n in where
    ]
    for copy in rows:
        copy.start()
    copies = tile_copies(own, sib, vals, sems, 0)
    for copy in copies:
        copy.start()
    out[...] = jnp.zeros_like(out)
    for copy in rows:
        copy.wait()
    for z in range(NZ):
        for x in range(NX):
            for b in range(4):
                hi, lo = split2(raw[z, x, b * SIDE : (b + 1) * SIDE])
                n = (z * NX + x) * 4 + b
                parts[n, :, :HALF] = hi
                parts[n, :, HALF:] = lo

    def run(base, live):
        def step(g, carry):
            terms = []
            for u in range(GROUP):
                q = base + g * GROUP + u
                terms.append(tile_dot(vals[q], parts[obj[q]]) * scale[pl.ds(q, 1), :])
            for u in range(GROUP):
                out[sub[base + g * GROUP + u]] += terms[u]
            return carry

        lax.fori_loop(0, (live + GROUP - 1) // GROUP, step, 0)

    for k, copy in enumerate(copies):
        copy.wait()
        core, first_tile = divmod(k * CHUNK, tiles)
        run(k * CHUNK, jnp.clip(cnt[core] - first_tile, 0, CHUNK))


def object_kernel(cnt, sub, obj, scale, rows, own, sib, acc, parts, vals, sems):
    tiles = own.shape[0]
    copies = tile_copies(own, sib, vals, sems, 0)
    for copy in copies:
        copy.start()
    acc[...] = jnp.zeros_like(acc)
    for b in range(4):
        hi, lo = split2(rows[b])
        parts[b, :, :HALF] = hi
        parts[b, :, HALF:] = lo

    def run(base, live):
        def step(g, carry):
            terms = []
            for u in range(GROUP):
                q = base + g * GROUP + u
                terms.append(tile_dot(vals[q].T, parts[sub[q]]) * scale[pl.ds(q, 1), :])
            for u in range(GROUP):
                at = pl.multiple_of(obj[base + g * GROUP + u] * SIDE, SIDE)
                acc[pl.ds(at, SIDE), :] += terms[u]
            return carry

        lax.fori_loop(0, (live + GROUP - 1) // GROUP, step, 0)

    for k, copy in enumerate(copies):
        copy.wait()
        core, first_tile = divmod(k * CHUNK, tiles)
        run(k * CHUNK, jnp.clip(cnt[core] - first_tile, 0, CHUNK))


SMEM = pl.BlockSpec(memory_space=pltpu.SMEM)
VMEM = pl.BlockSpec(memory_space=pltpu.VMEM)
HBM = pl.BlockSpec(memory_space=pltpu.HBM)


def subject_terms(cnt, sub, obj, scale, own, sib, pieces):
    return pl.pallas_call(
        functools.partial(subject_kernel, [where for _, where in pieces]),
        in_specs=[SMEM] * 3 + [VMEM] + [HBM] * (2 + len(pieces)),
        out_specs=VMEM,
        out_shape=jax.ShapeDtypeStruct((4, SIDE, HALF), F32),
        scratch_shapes=[
            pltpu.VMEM((NZ, NX, CHIP_ROWS, HALF), F32),
            pltpu.VMEM((BLOCKS, SIDE, 2 * HALF), BF),
            pltpu.VMEM((2 * own.shape[0], SIDE, SIDE), F32),
            pltpu.SemaphoreType.DMA((ROW_SEM + 1,)),
        ],
        compiler_params=pltpu.CompilerParams(vmem_limit_bytes=32 << 20),
        name="subject_terms",
    )(cnt, sub, obj, scale, own, sib, *[v for v, _ in pieces])


def object_terms(cnt, sub, obj, scale, rows, own, sib):
    return pl.pallas_call(
        object_kernel,
        in_specs=[SMEM] * 3 + [VMEM] * 2 + [HBM] * 2,
        out_specs=VMEM,
        out_shape=jax.ShapeDtypeStruct((BLOCKS * SIDE, HALF), F32),
        scratch_shapes=[
            pltpu.VMEM((4, SIDE, 2 * HALF), BF),
            pltpu.VMEM((2 * own.shape[0], SIDE, SIDE), F32),
            pltpu.SemaphoreType.DMA((2 * own.shape[0] // CHUNK,)),
        ],
        compiler_params=pltpu.CompilerParams(vmem_limit_bytes=32 << 20),
        name="object_terms",
    )(cnt, sub, obj, scale, rows, own, sib)


def body(
    tile_values,
    tile_subject,
    tile_object,
    tile_relation,
    tile_day,
    tile_count,
    object_factor,
    relation_factor,
    day_factor,
):
    s = lax.axis_index("subj")
    d = lax.axis_index("day")
    c = s % 2
    here_x = s // 2 % NX
    here_z = s // 8
    own = tile_values[0]
    tiles = own.shape[0]

    meta = jnp.concatenate(
        [
            tile_subject + 2 * c,
            tile_object,
            tile_relation,
            tile_day,
            jnp.broadcast_to(tile_count, (1, tiles)),
        ],
        0,
    )
    unit = to_chip(object_factor, c)
    meta2 = flip(meta, 1)

    gram = pack(gram_part(object_factor, d))
    unit, meta2, gram = lax.optimization_barrier((unit, meta2, gram + flip(gram, 1)))
    pieces, sib, gram, days = gather_rows(unit, gram, own, d, day_factor)

    sub = jnp.concatenate([meta[0], meta2[0]])
    obj = jnp.concatenate([meta[1], meta2[1]])
    rel = jnp.concatenate([meta[2], meta2[2]])
    day = jnp.concatenate([meta[3], meta2[3]])
    cnt = jnp.concatenate([meta[4, :1], meta2[4, :1]])
    p = obj // 2
    off_z = (p // 8 - here_z) % NZ
    off_x = (p // 2 % NX - here_x) % NX
    slot = ((off_z * NX + off_x) * 2 + p % 2) * 2 + obj % 2
    k = jnp.arange(tiles)
    live = jnp.concatenate([k < cnt[0], k < cnt[1]])
    rel_cols = lax.dynamic_slice_in_dim(relation_factor, c * HALF, HALF, 1)
    day_cols = lax.dynamic_slice_in_dim(day_factor, c * HALF, HALF, 1)
    rel_pick = (rel[:, None] == jnp.arange(relation_factor.shape[0])[None, :]).astype(F32)
    day_pick = (day[:, None] == jnp.arange(day_factor.shape[0])[None, :]).astype(F32)
    scale = jnp.dot(rel_pick, rel_cols, precision=HIGH) * jnp.dot(
        day_pick, day_cols, precision=HIGH
    )
    scale = scale * live[:, None].astype(F32)

    gram_rest = jnp.dot(relation_factor.T, relation_factor, precision=HIGH) * jnp.dot(
        days.T, days, precision=HIGH
    )
    gram_first = gram * gram_rest

    part = subject_terms(cnt, sub, slot, scale, own, sib, pieces)
    part, gram_first = lax.optimization_barrier((part, gram_first))
    total = day_sum(to_core(part.reshape(CHIP_ROWS, HALF), c))
    inv_first = inverse_factor(gram_first)
    raw = solve_rows(total, inv_first)
    lifted = raw * LIFT
    rows = to_chip(lifted, c).reshape(4, SIDE, HALF)

    gram = pack(gram_part(lifted, d))
    gram = gram + flip(gram, 1)
    rows, gram = lax.optimization_barrier((rows, gram))
    back = object_terms(cnt, sub, slot, scale, rows, own, sib)
    back = back.reshape(NZ, NX, CHIP_ROWS, HALF)
    rows, gram = scatter_rows(back, gram, d)
    gram_second = gram * gram_rest
    total = day_sum(to_core(rows, c))
    inv_second = inverse_factor(gram_second)
    raw_b = solve_rows(total, inv_second)

    tops = jnp.stack([jnp.max(jnp.abs(raw), axis=0), jnp.max(jnp.abs(raw_b), axis=0)])
    spread = jnp.broadcast_to(tops[None], (64,) + tops.shape)
    tops = jnp.max(lax.all_to_all(spread, "subj", 0, 0, tiled=True), axis=0)
    fall = tops[0] + EPS
    grown = fall * LIFT
    return (raw / fall, raw_b * (grown / (tops[1] * grown + EPS)))


def solution(mesh):
    return jax.shard_map(
        body,
        mesh=mesh,
        in_specs=(
            P("day", "subj", None, None),
            P("day", "subj"),
            P("day", "subj"),
            P("day", "subj"),
            P("day", "subj"),
            P("day", "subj"),
            P("subj", None),
            P(),
            P("day", None),
        ),
        out_specs=(P("subj", None), P("subj", None)),
        check_vma=False,
    )
```

```python
import functools

import jax
import jax.numpy as jnp
from jax import lax
from jax.experimental import pallas as pl
from jax.experimental.pallas import tpu as pltpu
from jax.sharding import PartitionSpec as P

F32 = jnp.float32
BF = jnp.bfloat16
HIGH = lax.Precision.HIGHEST
EPS = 1e-06
LIFT = 65536.0

NZ, NX = 8, 4
N_DAY = 4
SIDE = 128
HALF = 128
CHIP_ROWS = 512
SPLIT_X = 224
SPLIT_Z = CHIP_ROWS - SPLIT_X
BLOCKS = NZ * NX * 4
STRIP = 16
PANEL = 64
GROUP = 12
CHUNK = 48
ROW_SEM = 4


def pairs_z(k):
    return [(s, ((s // 8 + k) % NZ) * 8 + s % 8) for s in range(64)]


def pairs_x(k):
    return [(s, (s // 8) * 8 + ((s // 2 % 4 + k) % NX) * 2 + s % 2) for s in range(64)]


def flip(x, mask):
    return lax.ppermute(x, "subj", [(s, s ^ mask) for s in range(64)])


def flip_day(x, mask):
    return lax.ppermute(x, "day", [(s, s ^ mask) for s in range(N_DAY)])


def step(moves, *keep):
    got = [
        lax.ppermute(v, "subj", pairs) if axis == "subj" else flip_day(v, pairs)
        for v, axis, pairs in moves
    ]
    return lax.optimization_barrier((got, keep))


def xup(v):
    return (v, "subj", pairs_x(1))


def xdown(v):
    return (v, "subj", pairs_x(-1))


def zup(v):
    return (v, "subj", pairs_z(1))


def zdown(v):
    return (v, "subj", pairs_z(-1))


def mate(v, mask):
    return (v, "subj", [(s, s ^ mask) for s in range(64)])


def day_mate(v, mask):
    return (v, "day", mask)


def cut(v):
    h = v.shape[0] // 2
    return v[:h], v[h:]


def stack(*parts):
    return jnp.concatenate(parts, 0)


def pack(g):
    return stack(g[:, :HALF], g[:, HALF:])


def unpack(p):
    n = p.shape[0] // 2
    return jnp.concatenate([p[:n], p[n:]], 1)


def gather_rows(unit, gram, own, d, days):
    a, b = unit[:SPLIT_X], unit[SPLIT_X:]
    na, nb = SPLIT_X, SPLIT_Z
    m = stack(b, gram)
    (au, ad, bu1, bd1), (a,) = step([xup(a), xdown(a), zup(m), zdown(m)], a)
    (at, ab, bu2, bd2), (own,) = step(
        [xup(cut(au)[0]), xdown(cut(ad)[1]), zup(bu1), zdown(bd1)], own
    )
    sib = flip(own, 1)
    (bu3, bd3), () = step([zup(bu2), zdown(bd2)])
    h = nb // 2
    (bt, bb), (sib,) = step([zup(stack(bu3[:h], bu3[nb:])), zdown(bd3[h:nb])], sib)
    gram = gram + bu1[nb:] + bd1[nb:] + bu2[nb:] + bd2[nb:] + bu3[nb:] + bd3[nb:] + bt[h:]
    a = stack(a, ad, at, ab, au)
    w = 4 * nb
    low = stack(b, bd1[:nb], bd2[:nb], bd3[:nb], gram)
    m = stack(low, bt[:h], bb, bu3[:nb], bu2[:nb], bu1[:nb])
    a, m, gram = lax.optimization_barrier((a, m, gram))
    (xu, xd) = [lax.ppermute(m, "subj", pairs_x(k)) for k in (1, -1)]
    (au1, ad1), () = step([zup(a), zdown(a)])
    (au2, ad2), (xu, xd, gram) = step([zup(au1), zdown(ad1)], xu, xd, gram)
    fu = lax.ppermute(xu[: w + HALF], "subj", pairs_x(1))
    fd = lax.ppermute(xd[w + HALF :], "subj", pairs_x(-1))
    (au3, ad3), (gram,) = step([zup(au2), zdown(ad2)], gram)
    (at, ab), (fu, fd, gram) = step([zup(cut(au3)[0]), zdown(cut(ad3)[1])], fu, fd, gram)
    gram = unpack(gram + xu[w : w + HALF] + xd[w : w + HALF] + fu[w:])
    for mask in (1, 2):
        n = gram.shape[0]
        g = flip_day(stack(gram, days), mask)
        gram = day_join(gram, g[:n], d // mask % 2)
        days = day_join(days, g[n:], d // mask % 2)
    pieces = []
    for z, v in ((0, a), (1, ad1), (2, ad2), (3, ad3), (5, au3), (6, au2), (7, au1)):
        pieces.append((v, [(z, x, 0, x * na, na) for x in range(NX)]))
    for v, first in ((at, 0), (ab, 2)):
        pieces.append((v, [(4, first + x, 0, x * na, na) for x in range(2)]))
    for x, v in ((0, m), (3, xu), (1, xd)):
        where = [(z, x, na, z * nb, nb) for z in range(4)]
        pieces.append((v, where + [(4 + z, x, na, w + HALF + z * nb, nb) for z in range(4)]))
    for v, first in ((fu, 0), (fd, 4)):
        pieces.append((v, [(first + z, 2, na, z * nb, nb) for z in range(4)]))
    return pieces, sib, gram, days


def scatter_rows(back, gram, d):
    def to_z(z):
        return back[z, :, :SPLIT_X].reshape(NX * SPLIT_X, HALF)

    def to_x(x, first):
        return back[first : first + 4, x, SPLIT_X:].reshape(4 * SPLIT_Z, HALF)

    n = NX * SPLIT_X
    h = n // 2
    far_top, far_low = cut(to_z(4))
    w = 4 * SPLIT_Z
    (u, v, lu, hd), (gram,) = step(
        [zup(stack(far_top, gram)), zdown(stack(far_low, gram)), xup(to_x(2, 0)), xdown(to_x(2, 4))],
        gram,
    )
    xu = lax.ppermute(stack(to_x(1, 0) + lu, to_x(1, 4)), "subj", pairs_x(1))
    xd = lax.ppermute(stack(to_x(3, 0), to_x(3, 4) + hd), "subj", pairs_x(-1))
    gram = gram + u[h:] + v[h:]
    p, q = to_z(3), to_z(5)
    p = stack(p[:h] + u[:h], p[h:], u[h:])
    q = stack(q[:h], q[h:] + v[:h], v[h:])
    (u, v), (gram,) = step([zup(p), zdown(q)], gram)
    gram = gram + u[n:] + v[n:]
    p = stack(to_z(2) + u[:n], u[n:])
    q = stack(to_z(6) + v[:n], v[n:])
    (u, v), (gram, xu, xd) = step([zup(p), zdown(q)], gram, xu, xd)
    gram = gram + u[n:] + v[n:]
    low = to_x(0, 0) + xu[:w] + xd[:w]
    high = to_x(0, 4) + xu[w:] + xd[w:]
    b = [low[k * SPLIT_Z : (k + 1) * SPLIT_Z] for k in range(4)]
    b += [high[k * SPLIT_Z : (k + 1) * SPLIT_Z] for k in range(4)]
    p = stack(to_z(1) + u[:n], u[n:])
    q = to_z(7) + v[:n]
    (u, v, bu, bv), (gram, b) = step(
        [zup(p), zdown(q), zup(cut(b[4])[0]), zdown(cut(b[4])[1])], gram, b
    )
    gram = unpack(gram + u[n:])
    a = to_z(0) + u[:n] + v
    a = [a[k * SPLIT_X : (k + 1) * SPLIT_X] for k in range(NX)]
    p = stack(cut(b[3])[0] + bu, cut(b[3])[1])
    q = stack(cut(b[5])[0], cut(b[5])[1] + bv)
    (bu, bv, u, v, g), (gram, a, b) = step(
        [zup(p), zdown(q), xup(cut(a[2])[0]), xdown(cut(a[2])[1]), day_mate(gram, 1)], gram, a, b
    )
    gram = day_join(gram, g, d % 2)
    p = stack(cut(a[1])[0] + u, cut(a[1])[1])
    q = stack(cut(a[3])[0], cut(a[3])[1] + v)
    (bu, bv, u, v, g), (gram, a, b) = step(
        [zup(b[2] + bu), zdown(b[6] + bv), xup(p), xdown(q), day_mate(gram, 2)], gram, a, b
    )
    gram = day_join(gram, g, d // 2)
    a = a[0] + u + v
    (bu, bv), (a, b) = step([zup(b[1] + bu), zdown(b[7] + bv)], a, b)
    return stack(a, b[0] + bu + bv), gram


def day_join(mine, moved, late):
    return jnp.where(
        late == 1, jnp.concatenate([moved, mine], 0), jnp.concatenate([mine, moved], 0)
    )


def day_sum(x):
    return (x + flip_day(x, 1)) + (flip_day(x, 2) + flip_day(x, 3))


def core_order(c, mine, other, axis):
    return jnp.where(
        c == 0,
        jnp.concatenate([mine, other], axis),
        jnp.concatenate([other, mine], axis),
    )


def to_chip(m, c):
    mine = lax.dynamic_slice_in_dim(m, c * HALF, HALF, 1)
    send = lax.dynamic_slice_in_dim(m, (1 - c) * HALF, HALF, 1)
    return core_order(c, mine, flip(send, 1), 0)


def to_core(u, c):
    rows = CHIP_ROWS // 2
    mine = lax.dynamic_slice_in_dim(u, c * rows, rows, 0)
    send = lax.dynamic_slice_in_dim(u, (1 - c) * rows, rows, 0)
    return core_order(c, mine, flip(send, 1), 1)


def gram_part(m, d):
    quarter = m.shape[1] // N_DAY
    cols = lax.dynamic_slice_in_dim(m, d * quarter, quarter, 1)
    return jnp.dot(cols.T, m, precision=HIGH)


def exact_dot(a, b):
    return jnp.dot(a, b, precision=HIGH, preferred_element_type=F32)


def unit_matrix(n):
    i = lax.broadcasted_iota(jnp.int32, (n, n), 0)
    return (i == lax.broadcasted_iota(jnp.int32, (n, n), 1)).astype(F32)


def block_inverse(block):
    n = block.shape[0]
    wide = jnp.concatenate([block, unit_matrix(n)], 1)
    place = lax.broadcasted_iota(jnp.int32, wide.shape, 0)
    for p in range(0, n, STRIP):
        cols = [jnp.broadcast_to(wide[:, p + j : p + j + 1], wide.shape) for j in range(STRIP)]
        for j in range(STRIP):
            k = p + j
            pivot = cols[j][k : k + 1, :]
            r = lax.rsqrt(pivot)
            r = r * (1.5 - 0.5 * (pivot * r) * r)
            col = cols[j] * r
            row = wide[k : k + 1, :] * r
            below = jnp.where(place > k, col, 0.0)
            wide = jnp.where(place == k, row, wide - below * row)
            for t in range(j + 1, STRIP):
                cols[t] = cols[t] - below * col[p + t : p + t + 1, :]
    return wide[:, n:]


def factor_kernel(gram, out, work):
    n = gram.shape[0]
    work[...] = gram[...]
    out[...] = unit_matrix(n)
    for b in range(0, n, PANEL):
        e = b + PANEL
        inv = block_inverse(work[b:e, b:e])
        used = -(-e // 128) * 128
        top = exact_dot(inv, out[b:e, :used])
        out[b:e, :used] = top
        if e < n:
            panel = lax.dot_general(
                work[e:n, b:e], inv, (((1,), (1,)), ((), ())), precision=HIGH,
                preferred_element_type=F32,
            )
            work[e:n, e:n] -= lax.dot_general(
                panel, panel, (((1,), (1,)), ((), ())), precision=HIGH,
                preferred_element_type=F32,
            )
            out[e:n, :used] -= exact_dot(panel, top)


def inverse_factor(gram):
    return pl.pallas_call(
        factor_kernel,
        out_shape=jax.ShapeDtypeStruct(gram.shape, F32),
        scratch_shapes=[pltpu.VMEM(gram.shape, F32)],
        name="inverse_factor",
    )(gram)


def solve_rows(total, inv):
    y = jnp.dot(total, inv.T, precision=HIGH)
    return jnp.dot(y, inv, precision=HIGH)


def split2(x):
    hi = x.astype(BF)
    lo = (x - hi.astype(F32)).astype(BF)
    return hi, lo


def tile_dot(v, w):
    hi, lo = split2(v)
    r = jnp.dot(
        jnp.concatenate([hi, lo], 1), jnp.concatenate([w, w], 0), preferred_element_type=F32
    )
    return r[:, :HALF] + r[:, HALF:]


def tile_copies(own, sib, vals, sems, first_sem):
    tiles = own.shape[0]
    copies = []
    for core, src in enumerate((own, sib)):
        for at in range(0, tiles, CHUNK):
            copies.append(
                pltpu.make_async_copy(
                    src.at[pl.ds(at, CHUNK)],
                    vals.at[pl.ds(core * tiles + at, CHUNK)],
                    sems.at[first_sem + len(copies)],
                )
            )
    return copies


def subject_kernel(places, cnt, sub, obj, scale, own, sib, *rest):
    pieces = rest[: len(places)]
    out, raw, parts, vals, sems = rest[len(places) :]
    tiles = own.shape[0]
    rows = [
        pltpu.make_async_copy(
            ref.at[pl.ds(here, n)], raw.at[z, x, pl.ds(there, n)], sems.at[ROW_SEM]
        )
        for ref, where in zip(pieces, places)
        for z, x, there, here, n in where
    ]
    for copy in rows:
        copy.start()
    copies = tile_copies(own, sib, vals, sems, 0)
    for copy in copies:
        copy.start()
    out[...] = jnp.zeros_like(out)
    for copy in rows:
        copy.wait()
    for z in range(NZ):
        for x in range(NX):
            for b in range(4):
                hi, lo = split2(raw[z, x, b * SIDE : (b + 1) * SIDE])
                n = (z * NX + x) * 4 + b
                parts[n, :, :HALF] = hi
                parts[n, :, HALF:] = lo

    def run(base, live):
        def step(g, carry):
            terms = []
            for u in range(GROUP):
                q = base + g * GROUP + u
                terms.append(tile_dot(vals[q], parts[obj[q]]) * scale[pl.ds(q, 1), :])
            for u in range(GROUP):
                out[sub[base + g * GROUP + u]] += terms[u]
            return carry

        lax.fori_loop(0, (live + GROUP - 1) // GROUP, step, 0)

    for k, copy in enumerate(copies):
        copy.wait()
        core, first_tile = divmod(k * CHUNK, tiles)
        run(k * CHUNK, jnp.clip(cnt[core] - first_tile, 0, CHUNK))


def object_kernel(cnt, sub, obj, scale, rows, own, sib, acc, parts, vals, sems):
    tiles = own.shape[0]
    copies = tile_copies(own, sib, vals, sems, 0)
    for copy in copies:
        copy.start()
    acc[...] = jnp.zeros_like(acc)
    for b in range(4):
        hi, lo = split2(rows[b])
        parts[b, :, :HALF] = hi
        parts[b, :, HALF:] = lo

    def run(base, live):
        def step(g, carry):
            terms = []
            for u in range(GROUP):
                q = base + g * GROUP + u
                terms.append(tile_dot(vals[q].T, parts[sub[q]]) * scale[pl.ds(q, 1), :])
            for u in range(GROUP):
                at = pl.multiple_of(obj[base + g * GROUP + u] * SIDE, SIDE)
                acc[pl.ds(at, SIDE), :] += terms[u]
            return carry

        lax.fori_loop(0, (live + GROUP - 1) // GROUP, step, 0)

    for k, copy in enumerate(copies):
        copy.wait()
        core, first_tile = divmod(k * CHUNK, tiles)
        run(k * CHUNK, jnp.clip(cnt[core] - first_tile, 0, CHUNK))


SMEM = pl.BlockSpec(memory_space=pltpu.SMEM)
VMEM = pl.BlockSpec(memory_space=pltpu.VMEM)
HBM = pl.BlockSpec(memory_space=pltpu.HBM)


def subject_terms(cnt, sub, obj, scale, own, sib, pieces):
    return pl.pallas_call(
        functools.partial(subject_kernel, [where for _, where in pieces]),
        in_specs=[SMEM] * 3 + [VMEM] + [HBM] * (2 + len(pieces)),
        out_specs=VMEM,
        out_shape=jax.ShapeDtypeStruct((4, SIDE, HALF), F32),
        scratch_shapes=[
            pltpu.VMEM((NZ, NX, CHIP_ROWS, HALF), F32),
            pltpu.VMEM((BLOCKS, SIDE, 2 * HALF), BF),
            pltpu.VMEM((2 * own.shape[0], SIDE, SIDE), F32),
            pltpu.SemaphoreType.DMA((ROW_SEM + 1,)),
        ],
        compiler_params=pltpu.CompilerParams(vmem_limit_bytes=32 << 20),
        name="subject_terms",
    )(cnt, sub, obj, scale, own, sib, *[v for v, _ in pieces])


def object_terms(cnt, sub, obj, scale, rows, own, sib):
    return pl.pallas_call(
        object_kernel,
        in_specs=[SMEM] * 3 + [VMEM] * 2 + [HBM] * 2,
        out_specs=VMEM,
        out_shape=jax.ShapeDtypeStruct((BLOCKS * SIDE, HALF), F32),
        scratch_shapes=[
            pltpu.VMEM((4, SIDE, 2 * HALF), BF),
            pltpu.VMEM((2 * own.shape[0], SIDE, SIDE), F32),
            pltpu.SemaphoreType.DMA((2 * own.shape[0] // CHUNK,)),
        ],
        compiler_params=pltpu.CompilerParams(vmem_limit_bytes=32 << 20),
        name="object_terms",
    )(cnt, sub, obj, scale, rows, own, sib)


def body(
    tile_values,
    tile_subject,
    tile_object,
    tile_relation,
    tile_day,
    tile_count,
    object_factor,
    relation_factor,
    day_factor,
):
    s = lax.axis_index("subj")
    d = lax.axis_index("day")
    c = s % 2
    here_x = s // 2 % NX
    here_z = s // 8
    own = tile_values[0]
    tiles = own.shape[0]

    meta = jnp.concatenate(
        [
            tile_subject + 2 * c,
            tile_object,
            tile_relation,
            tile_day,
            jnp.broadcast_to(tile_count, (1, tiles)),
        ],
        0,
    )
    unit = to_chip(object_factor, c)
    meta2 = flip(meta, 1)

    gram = pack(gram_part(object_factor, d))
    unit, meta2, gram = lax.optimization_barrier((unit, meta2, gram + flip(gram, 1)))
    pieces, sib, gram, days = gather_rows(unit, gram, own, d, day_factor)

    sub = jnp.concatenate([meta[0], meta2[0]])
    obj = jnp.concatenate([meta[1], meta2[1]])
    rel = jnp.concatenate([meta[2], meta2[2]])
    day = jnp.concatenate([meta[3], meta2[3]])
    cnt = jnp.concatenate([meta[4, :1], meta2[4, :1]])
    p = obj // 2
    off_z = (p // 8 - here_z) % NZ
    off_x = (p // 2 % NX - here_x) % NX
    slot = ((off_z * NX + off_x) * 2 + p % 2) * 2 + obj % 2
    k = jnp.arange(tiles)
    live = jnp.concatenate([k < cnt[0], k < cnt[1]])
    rel_cols = lax.dynamic_slice_in_dim(relation_factor, c * HALF, HALF, 1)
    day_cols = lax.dynamic_slice_in_dim(day_factor, c * HALF, HALF, 1)
    rel_pick = (rel[:, None] == jnp.arange(relation_factor.shape[0])[None, :]).astype(F32)
    day_pick = (day[:, None] == jnp.arange(day_factor.shape[0])[None, :]).astype(F32)
    scale = jnp.dot(rel_pick, rel_cols, precision=HIGH) * jnp.dot(
        day_pick, day_cols, precision=HIGH
    )
    scale = scale * live[:, None].astype(F32)

    gram_rest = jnp.dot(relation_factor.T, relation_factor, precision=HIGH) * jnp.dot(
        days.T, days, precision=HIGH
    )
    gram_first = gram * gram_rest

    part = subject_terms(cnt, sub, slot, scale, own, sib, pieces)
    part, gram_first = lax.optimization_barrier((part, gram_first))
    total = day_sum(to_core(part.reshape(CHIP_ROWS, HALF), c))
    inv_first = inverse_factor(gram_first)
    raw = solve_rows(total, inv_first)
    lifted = raw * LIFT
    rows = to_chip(lifted, c).reshape(4, SIDE, HALF)

    gram = pack(gram_part(lifted, d))
    gram = gram + flip(gram, 1)
    rows, gram = lax.optimization_barrier((rows, gram))
    moved = [flip(gram, mask) for mask in (2, 4, 6)]
    back = object_terms(cnt, sub, slot, scale, rows, own, sib)
    back, gram, moved = lax.optimization_barrier((back, gram, moved))
    back = back.reshape(NZ, NX, CHIP_ROWS, HALF)
    rows, gram = scatter_rows(back, (gram + moved[0]) + (moved[1] + moved[2]), d)
    gram_second = gram * gram_rest
    rows, gram_second = lax.optimization_barrier((rows, gram_second))
    total = day_sum(to_core(rows, c))
    inv_second = inverse_factor(gram_second)
    raw_b = solve_rows(total, inv_second)

    tops = jnp.stack([jnp.max(jnp.abs(raw), axis=0), jnp.max(jnp.abs(raw_b), axis=0)])
    spread = jnp.broadcast_to(tops[None], (64,) + tops.shape)
    tops = jnp.max(lax.all_to_all(spread, "subj", 0, 0, tiled=True), axis=0)
    fall = tops[0] + EPS
    grown = fall * LIFT
    return (raw / fall, raw_b * (grown / (tops[1] * grown + EPS)))


def solution(mesh):
    return jax.shard_map(
        body,
        mesh=mesh,
        in_specs=(
            P("day", "subj", None, None),
            P("day", "subj"),
            P("day", "subj"),
            P("day", "subj"),
            P("day", "subj"),
            P("day", "subj"),
            P("subj", None),
            P(),
            P("day", None),
        ),
        out_specs=(P("subj", None), P("subj", None)),
        check_vma=False,
    )
```

```python
import functools

import jax
import jax.numpy as jnp
from jax import lax
from jax.experimental import pallas as pl
from jax.experimental.pallas import tpu as pltpu
from jax.sharding import PartitionSpec as P

F32 = jnp.float32
BF = jnp.bfloat16
HIGH = lax.Precision.HIGHEST
EPS = 1e-06
LIFT = 65536.0

NZ, NX = 8, 4
N_DAY = 4
SIDE = 128
HALF = 128
CHIP_ROWS = 512
SPLIT_X = 224
SPLIT_Z = CHIP_ROWS - SPLIT_X
BLOCKS = NZ * NX * 4
STRIP = 16
PANEL = 64
GROUP = 12
CHUNK = 48
ROW_SEM = 4


def pairs_z(k):
    return [(s, ((s // 8 + k) % NZ) * 8 + s % 8) for s in range(64)]


def pairs_x(k):
    return [(s, (s // 8) * 8 + ((s // 2 % 4 + k) % NX) * 2 + s % 2) for s in range(64)]


def flip(x, mask):
    return lax.ppermute(x, "subj", [(s, s ^ mask) for s in range(64)])


def flip_day(x, mask):
    return lax.ppermute(x, "day", [(s, s ^ mask) for s in range(N_DAY)])


def step(moves, *keep):
    got = [
        lax.ppermute(v, "subj", pairs) if axis == "subj" else flip_day(v, pairs)
        for v, axis, pairs in moves
    ]
    return lax.optimization_barrier((got, keep))


def xup(v):
    return (v, "subj", pairs_x(1))


def xdown(v):
    return (v, "subj", pairs_x(-1))


def zup(v):
    return (v, "subj", pairs_z(1))


def zdown(v):
    return (v, "subj", pairs_z(-1))


def mate(v, mask):
    return (v, "subj", [(s, s ^ mask) for s in range(64)])


def day_mate(v, mask):
    return (v, "day", mask)


def cut(v):
    h = v.shape[0] // 2
    return v[:h], v[h:]


def stack(*parts):
    return jnp.concatenate(parts, 0)


def pack(g):
    return stack(g[:, :HALF], g[:, HALF:])


def unpack(p):
    n = p.shape[0] // 2
    return jnp.concatenate([p[:n], p[n:]], 1)


def gather_rows(unit, gram, own, d, days):
    a, b = unit[:SPLIT_X], unit[SPLIT_X:]
    na, nb = SPLIT_X, SPLIT_Z
    m = stack(b, gram)
    (au, ad, bu1, bd1), (a,) = step([xup(a), xdown(a), zup(m), zdown(m)], a)
    (at, ab, bu2, bd2), (own,) = step(
        [xup(cut(au)[0]), xdown(cut(ad)[1]), zup(bu1), zdown(bd1)], own
    )
    sib = flip(own, 1)
    (bu3, bd3), () = step([zup(bu2), zdown(bd2)])
    h = nb // 2
    (bt, bb), (sib,) = step([zup(stack(bu3[:h], bu3[nb:])), zdown(bd3[h:nb])], sib)
    gram = gram + bu1[nb:] + bd1[nb:] + bu2[nb:] + bd2[nb:] + bu3[nb:] + bd3[nb:] + bt[h:]
    a = stack(a, ad, at, ab, au)
    w = 4 * nb
    low = stack(b, bd1[:nb], bd2[:nb], bd3[:nb], gram)
    m = stack(low, bt[:h], bb, bu3[:nb], bu2[:nb], bu1[:nb])
    a, m, gram = lax.optimization_barrier((a, m, gram))
    (xu, xd) = [lax.ppermute(m, "subj", pairs_x(k)) for k in (1, -1)]
    (au1, ad1), () = step([zup(a), zdown(a)])
    (au2, ad2), (xu, xd, gram) = step([zup(au1), zdown(ad1)], xu, xd, gram)
    fu = lax.ppermute(xu[: w + HALF], "subj", pairs_x(1))
    fd = lax.ppermute(xd[w + HALF :], "subj", pairs_x(-1))
    (au3, ad3), (gram,) = step([zup(au2), zdown(ad2)], gram)
    (at, ab), (fu, fd, gram) = step([zup(cut(au3)[0]), zdown(cut(ad3)[1])], fu, fd, gram)
    gram = unpack(gram + xu[w : w + HALF] + xd[w : w + HALF] + fu[w:])
    for mask in (1, 2):
        n = gram.shape[0]
        g = flip_day(stack(gram, days), mask)
        gram = day_join(gram, g[:n], d // mask % 2)
        days = day_join(days, g[n:], d // mask % 2)
    pieces = []
    for z, v in ((0, a), (1, ad1), (2, ad2), (3, ad3), (5, au3), (6, au2), (7, au1)):
        pieces.append((v, [(z, x, 0, x * na, na) for x in range(NX)]))
    for v, first in ((at, 0), (ab, 2)):
        pieces.append((v, [(4, first + x, 0, x * na, na) for x in range(2)]))
    for x, v in ((0, m), (3, xu), (1, xd)):
        where = [(z, x, na, z * nb, nb) for z in range(4)]
        pieces.append((v, where + [(4 + z, x, na, w + HALF + z * nb, nb) for z in range(4)]))
    for v, first in ((fu, 0), (fd, 4)):
        pieces.append((v, [(first + z, 2, na, z * nb, nb) for z in range(4)]))
    return pieces, sib, gram, days


def scatter_rows(back, gram, d):
    def to_z(z):
        return back[z, :, :SPLIT_X].reshape(NX * SPLIT_X, HALF)

    def to_x(x, first):
        return back[first : first + 4, x, SPLIT_X:].reshape(4 * SPLIT_Z, HALF)

    n = NX * SPLIT_X
    h = n // 2
    far_top, far_low = cut(to_z(4))
    w = 4 * SPLIT_Z
    (u, v, lu, hd), (gram,) = step(
        [zup(stack(far_top, gram)), zdown(stack(far_low, gram)), xup(to_x(2, 0)), xdown(to_x(2, 4))],
        gram,
    )
    xu = lax.ppermute(stack(to_x(1, 0) + lu, to_x(1, 4)), "subj", pairs_x(1))
    xd = lax.ppermute(stack(to_x(3, 0), to_x(3, 4) + hd), "subj", pairs_x(-1))
    gram = gram + u[h:] + v[h:]
    p, q = to_z(3), to_z(5)
    p = stack(p[:h] + u[:h], p[h:], u[h:])
    q = stack(q[:h], q[h:] + v[:h], v[h:])
    (u, v), (gram,) = step([zup(p), zdown(q)], gram)
    gram = gram + u[n:] + v[n:]
    p = stack(to_z(2) + u[:n], u[n:])
    q = stack(to_z(6) + v[:n], v[n:])
    (u, v), (gram, xu, xd) = step([zup(p), zdown(q)], gram, xu, xd)
    gram = gram + u[n:] + v[n:]
    low = to_x(0, 0) + xu[:w] + xd[:w]
    high = to_x(0, 4) + xu[w:] + xd[w:]
    b = [low[k * SPLIT_Z : (k + 1) * SPLIT_Z] for k in range(4)]
    b += [high[k * SPLIT_Z : (k + 1) * SPLIT_Z] for k in range(4)]
    p = stack(to_z(1) + u[:n], u[n:])
    q = to_z(7) + v[:n]
    (u, v, bu, bv), (gram, b) = step(
        [zup(p), zdown(q), zup(cut(b[4])[0]), zdown(cut(b[4])[1])], gram, b
    )
    gram = unpack(gram + u[n:])
    a = to_z(0) + u[:n] + v
    a = [a[k * SPLIT_X : (k + 1) * SPLIT_X] for k in range(NX)]
    p = stack(cut(b[3])[0] + bu, cut(b[3])[1])
    q = stack(cut(b[5])[0], cut(b[5])[1] + bv)
    (bu, bv, u, v, g), (gram, a, b) = step(
        [zup(p), zdown(q), xup(cut(a[2])[0]), xdown(cut(a[2])[1]), day_mate(gram, 1)], gram, a, b
    )
    gram = day_join(gram, g, d % 2)
    p = stack(cut(a[1])[0] + u, cut(a[1])[1])
    q = stack(cut(a[3])[0], cut(a[3])[1] + v)
    (bu, bv, u, v, g), (gram, a, b) = step(
        [zup(b[2] + bu), zdown(b[6] + bv), xup(p), xdown(q), day_mate(gram, 2)], gram, a, b
    )
    gram = day_join(gram, g, d // 2)
    a = a[0] + u + v
    (bu, bv), (a, b) = step([zup(b[1] + bu), zdown(b[7] + bv)], a, b)
    return stack(a, b[0] + bu + bv), gram


def day_join(mine, moved, late):
    return jnp.where(
        late == 1, jnp.concatenate([moved, mine], 0), jnp.concatenate([mine, moved], 0)
    )


def day_sum(x):
    return (x + flip_day(x, 1)) + (flip_day(x, 2) + flip_day(x, 3))


def core_order(c, mine, other, axis):
    return jnp.where(
        c == 0,
        jnp.concatenate([mine, other], axis),
        jnp.concatenate([other, mine], axis),
    )


def to_chip(m, c):
    mine = lax.dynamic_slice_in_dim(m, c * HALF, HALF, 1)
    send = lax.dynamic_slice_in_dim(m, (1 - c) * HALF, HALF, 1)
    return core_order(c, mine, flip(send, 1), 0)


def to_core(u, c):
    rows = CHIP_ROWS // 2
    mine = lax.dynamic_slice_in_dim(u, c * rows, rows, 0)
    send = lax.dynamic_slice_in_dim(u, (1 - c) * rows, rows, 0)
    return core_order(c, mine, flip(send, 1), 1)


def gram_part(m, d):
    quarter = m.shape[1] // N_DAY
    cols = lax.dynamic_slice_in_dim(m, d * quarter, quarter, 1)
    return jnp.dot(cols.T, m, precision=HIGH)


def exact_dot(a, b):
    return jnp.dot(a, b, precision=HIGH, preferred_element_type=F32)


def unit_matrix(n):
    i = lax.broadcasted_iota(jnp.int32, (n, n), 0)
    return (i == lax.broadcasted_iota(jnp.int32, (n, n), 1)).astype(F32)


def block_inverse(block):
    n = block.shape[0]
    wide = jnp.concatenate([block, unit_matrix(n)], 1)
    place = lax.broadcasted_iota(jnp.int32, wide.shape, 0)
    for p in range(0, n, STRIP):
        cols = [jnp.broadcast_to(wide[:, p + j : p + j + 1], wide.shape) for j in range(STRIP)]
        for j in range(STRIP):
            k = p + j
            pivot = cols[j][k : k + 1, :]
            r = lax.rsqrt(pivot)
            r = r * (1.5 - 0.5 * (pivot * r) * r)
            col = cols[j] * r
            row = wide[k : k + 1, :] * r
            below = jnp.where(place > k, col, 0.0)
            wide = jnp.where(place == k, row, wide - below * row)
            for t in range(j + 1, STRIP):
                cols[t] = cols[t] - below * col[p + t : p + t + 1, :]
    return wide[:, n:]


def factor_kernel(gram, out, work):
    n = gram.shape[0]
    work[...] = gram[...]
    out[...] = unit_matrix(n)
    for b in range(0, n, PANEL):
        e = b + PANEL
        inv = block_inverse(work[b:e, b:e])
        used = -(-e // 128) * 128
        top = exact_dot(inv, out[b:e, :used])
        out[b:e, :used] = top
        if e < n:
            panel = lax.dot_general(
                work[e:n, b:e], inv, (((1,), (1,)), ((), ())), precision=HIGH,
                preferred_element_type=F32,
            )
            work[e:n, e:n] -= lax.dot_general(
                panel, panel, (((1,), (1,)), ((), ())), precision=HIGH,
                preferred_element_type=F32,
            )
            out[e:n, :used] -= exact_dot(panel, top)


def inverse_factor(gram):
    return pl.pallas_call(
        factor_kernel,
        out_shape=jax.ShapeDtypeStruct(gram.shape, F32),
        scratch_shapes=[pltpu.VMEM(gram.shape, F32)],
        name="inverse_factor",
    )(gram)


def solve_rows(total, inv):
    y = jnp.dot(total, inv.T, precision=HIGH)
    return jnp.dot(y, inv, precision=HIGH)


def split2(x):
    hi = x.astype(BF)
    lo = (x - hi.astype(F32)).astype(BF)
    return hi, lo


def tile_dot(v, w):
    hi, lo = split2(v)
    r = jnp.dot(
        jnp.concatenate([hi, lo], 1), jnp.concatenate([w, w], 0), preferred_element_type=F32
    )
    return r[:, :HALF] + r[:, HALF:]


def tile_copies(own, sib, vals, sems, first_sem):
    tiles = own.shape[0]
    copies = []
    for core, src in enumerate((own, sib)):
        for at in range(0, tiles, CHUNK):
            copies.append(
                pltpu.make_async_copy(
                    src.at[pl.ds(at, CHUNK)],
                    vals.at[pl.ds(core * tiles + at, CHUNK)],
                    sems.at[first_sem + len(copies)],
                )
            )
    return copies


def subject_kernel(places, cnt, sub, obj, scale, own, sib, *rest):
    pieces = rest[: len(places)]
    out, raw, parts, vals, sems = rest[len(places) :]
    tiles = own.shape[0]

    def rows(z):
        return [
            pltpu.make_async_copy(
                ref.at[pl.ds(here, n)], raw.at[z % 2, x, pl.ds(there, n)], sems.at[ROW_SEM + z % 2]
            )
            for ref, where in zip(pieces, places)
            for at, x, there, here, n in where
            if at == z
        ]

    for copy in rows(0):
        copy.start()
    copies = tile_copies(own, sib, vals, sems, 0)
    out[...] = jnp.zeros_like(out)
    for z in range(NZ):
        if z + 1 < NZ:
            for copy in rows(z + 1):
                copy.start()
        if z % 2 == 1:
            copies[z // 2].start()
        for copy in rows(z):
            copy.wait()
        for x in range(NX):
            for b in range(4):
                hi, lo = split2(raw[z % 2, x, b * SIDE : (b + 1) * SIDE])
                n = (z * NX + x) * 4 + b
                parts[n, :, :HALF] = hi
                parts[n, :, HALF:] = lo

    def run(base, live):
        def step(g, carry):
            terms = []
            for u in range(GROUP):
                q = base + g * GROUP + u
                terms.append(tile_dot(vals[q], parts[obj[q]]) * scale[pl.ds(q, 1), :])
            for u in range(GROUP):
                out[sub[base + g * GROUP + u]] += terms[u]
            return carry

        lax.fori_loop(0, (live + GROUP - 1) // GROUP, step, 0)

    for k, copy in enumerate(copies):
        copy.wait()
        core, first_tile = divmod(k * CHUNK, tiles)
        run(k * CHUNK, jnp.clip(cnt[core] - first_tile, 0, CHUNK))


def object_kernel(cnt, sub, obj, scale, rows, own, sib, acc, parts, vals, sems):
    tiles = own.shape[0]
    copies = tile_copies(own, sib, vals, sems, 0)
    for copy in copies:
        copy.start()
    acc[...] = jnp.zeros_like(acc)
    for b in range(4):
        hi, lo = split2(rows[b])
        parts[b, :, :HALF] = hi
        parts[b, :, HALF:] = lo

    def run(base, live):
        def step(g, carry):
            terms = []
            for u in range(GROUP):
                q = base + g * GROUP + u
                terms.append(tile_dot(vals[q].T, parts[sub[q]]) * scale[pl.ds(q, 1), :])
            for u in range(GROUP):
                at = pl.multiple_of(obj[base + g * GROUP + u] * SIDE, SIDE)
                acc[pl.ds(at, SIDE), :] += terms[u]
            return carry

        lax.fori_loop(0, (live + GROUP - 1) // GROUP, step, 0)

    for k, copy in enumerate(copies):
        copy.wait()
        core, first_tile = divmod(k * CHUNK, tiles)
        run(k * CHUNK, jnp.clip(cnt[core] - first_tile, 0, CHUNK))


SMEM = pl.BlockSpec(memory_space=pltpu.SMEM)
VMEM = pl.BlockSpec(memory_space=pltpu.VMEM)
HBM = pl.BlockSpec(memory_space=pltpu.HBM)


def subject_terms(cnt, sub, obj, scale, own, sib, pieces):
    return pl.pallas_call(
        functools.partial(subject_kernel, [where for _, where in pieces]),
        in_specs=[SMEM] * 3 + [VMEM] + [HBM] * (2 + len(pieces)),
        out_specs=VMEM,
        out_shape=jax.ShapeDtypeStruct((4, SIDE, HALF), F32),
        scratch_shapes=[
            pltpu.VMEM((2, NX, CHIP_ROWS, HALF), F32),
            pltpu.VMEM((BLOCKS, SIDE, 2 * HALF), BF),
            pltpu.VMEM((2 * own.shape[0], SIDE, SIDE), F32),
            pltpu.SemaphoreType.DMA((ROW_SEM + 2,)),
        ],
        compiler_params=pltpu.CompilerParams(vmem_limit_bytes=24 << 20),
        name="subject_terms",
    )(cnt, sub, obj, scale, own, sib, *[v for v, _ in pieces])


def object_terms(cnt, sub, obj, scale, rows, own, sib):
    return pl.pallas_call(
        object_kernel,
        in_specs=[SMEM] * 3 + [VMEM] * 2 + [HBM] * 2,
        out_specs=VMEM,
        out_shape=jax.ShapeDtypeStruct((BLOCKS * SIDE, HALF), F32),
        scratch_shapes=[
            pltpu.VMEM((4, SIDE, 2 * HALF), BF),
            pltpu.VMEM((2 * own.shape[0], SIDE, SIDE), F32),
            pltpu.SemaphoreType.DMA((2 * own.shape[0] // CHUNK,)),
        ],
        compiler_params=pltpu.CompilerParams(vmem_limit_bytes=24 << 20),
        name="object_terms",
    )(cnt, sub, obj, scale, rows, own, sib)


def body(
    tile_values,
    tile_subject,
    tile_object,
    tile_relation,
    tile_day,
    tile_count,
    object_factor,
    relation_factor,
    day_factor,
):
    s = lax.axis_index("subj")
    d = lax.axis_index("day")
    c = s % 2
    here_x = s // 2 % NX
    here_z = s // 8
    own = tile_values[0]
    tiles = own.shape[0]

    meta = jnp.concatenate(
        [
            tile_subject + 2 * c,
            tile_object,
            tile_relation,
            tile_day,
            jnp.broadcast_to(tile_count, (1, tiles)),
        ],
        0,
    )
    unit = to_chip(object_factor, c)
    meta2 = flip(meta, 1)

    gram = pack(gram_part(object_factor, d))
    unit, meta2, gram = lax.optimization_barrier((unit, meta2, gram + flip(gram, 1)))
    pieces, sib, gram, days = gather_rows(unit, gram, own, d, day_factor)

    sub = jnp.concatenate([meta[0], meta2[0]])
    obj = jnp.concatenate([meta[1], meta2[1]])
    rel = jnp.concatenate([meta[2], meta2[2]])
    day = jnp.concatenate([meta[3], meta2[3]])
    cnt = jnp.concatenate([meta[4, :1], meta2[4, :1]])
    p = obj // 2
    off_z = (p // 8 - here_z) % NZ
    off_x = (p // 2 % NX - here_x) % NX
    slot = ((off_z * NX + off_x) * 2 + p % 2) * 2 + obj % 2
    k = jnp.arange(tiles)
    live = jnp.concatenate([k < cnt[0], k < cnt[1]])
    rel_cols = lax.dynamic_slice_in_dim(relation_factor, c * HALF, HALF, 1)
    day_cols = lax.dynamic_slice_in_dim(day_factor, c * HALF, HALF, 1)
    rel_pick = (rel[:, None] == jnp.arange(relation_factor.shape[0])[None, :]).astype(F32)
    day_pick = (day[:, None] == jnp.arange(day_factor.shape[0])[None, :]).astype(F32)
    scale = jnp.dot(rel_pick, rel_cols, precision=HIGH) * jnp.dot(
        day_pick, day_cols, precision=HIGH
    )
    scale = scale * live[:, None].astype(F32)

    gram_rest = jnp.dot(relation_factor.T, relation_factor, precision=HIGH) * jnp.dot(
        days.T, days, precision=HIGH
    )
    gram_first = gram * gram_rest

    part = subject_terms(cnt, sub, slot, scale, own, sib, pieces)
    part, gram_first = lax.optimization_barrier((part, gram_first))
    total = day_sum(to_core(part.reshape(CHIP_ROWS, HALF), c))
    inv_first = inverse_factor(gram_first)
    raw = solve_rows(total, inv_first)
    lifted = raw * LIFT
    rows = to_chip(lifted, c).reshape(4, SIDE, HALF)

    gram = pack(gram_part(lifted, d))
    gram = gram + flip(gram, 1)
    rows, gram = lax.optimization_barrier((rows, gram))
    moved = [flip(gram, mask) for mask in (2, 4, 6)]
    back = object_terms(cnt, sub, slot, scale, rows, own, sib)
    back, gram, moved = lax.optimization_barrier((back, gram, moved))
    back = back.reshape(NZ, NX, CHIP_ROWS, HALF)
    rows, gram = scatter_rows(back, (gram + moved[0]) + (moved[1] + moved[2]), d)
    gram_second = gram * gram_rest
    rows, gram_second = lax.optimization_barrier((rows, gram_second))
    total = day_sum(to_core(rows, c))
    inv_second = inverse_factor(gram_second)
    raw_b = solve_rows(total, inv_second)

    tops = jnp.stack([jnp.max(jnp.abs(raw), axis=0), jnp.max(jnp.abs(raw_b), axis=0)])
    spread = jnp.broadcast_to(tops[None], (64,) + tops.shape)
    tops = jnp.max(lax.all_to_all(spread, "subj", 0, 0, tiled=True), axis=0)
    fall = tops[0] + EPS
    grown = fall * LIFT
    return (raw / fall, raw_b * (grown / (tops[1] * grown + EPS)))


def solution(mesh):
    return jax.shard_map(
        body,
        mesh=mesh,
        in_specs=(
            P("day", "subj", None, None),
            P("day", "subj"),
            P("day", "subj"),
            P("day", "subj"),
            P("day", "subj"),
            P("day", "subj"),
            P("subj", None),
            P(),
            P("day", None),
        ),
        out_specs=(P("subj", None), P("subj", None)),
        check_vma=False,
    )
```
